256 devices in a mesh: expert: 32 (over x, y, core), tensor: 8 (over z).
Axes of the slice: x: 4, y: 4, z: 8, core: 2. Of those that a mesh axis runs over, the one named last changes fastest.
Arguments:
- tokens: bfloat16 [32768, 8192], P(('expert', 'tensor')), may hold values from -6 to 6
- routes: int32 [32768, 2], P(('expert', 'tensor')), may hold values from 0 to 63, all different within a row; in each aligned block of 128 rows (0 to 127, 128 to 255, ...) at most 8 rows name the same one
- route_weight: float32 [32768, 2], P(('expert', 'tensor')), may hold values from 0.1 to 1
- shrink_weight: bfloat16 [64, 32, 8192], P('expert'), may hold values from -0.0625 to 0.0625
- expand_weight: bfloat16 [64, 32, 8192], P('expert', None, 'tensor'), may hold values from -1 to 1
Outputs:
- adapted: bfloat16 [32768, 8192], P(('expert', 'tensor'))
The draws below stay inside these ranges and needn't reach their ends.
Inputs may be any that keep to these rules, and one draw needn't show every extreme that they name: `routes`: in each aligned block of 128 rows (the tokens of one device) a row names two different experts and no expert is named by more than 8 rows; in every draw some expert is named by exactly 8 rows of some block.
All inputs are finite; a program needn't handle non-finite values.
Results may differ from the reference program's by a relative error of at most 0.0058.
Values may be sent and summed in bfloat16 or wider, within the bound.
No kernel may reach another device: no remote copies, remote signals or barrier semaphores. Data moves between devices by JAX's collectives and lax.ppermute only.
A program may use at most 128 MiB of HBM per device.

```python
import math
import jax
import jax.numpy as jnp
import numpy as np
from jax import lax

D = 8192
EXPERTS = 64
R = 32
TOK_DEV = 128
CAP = 8
TOKENS = 32768


def levels(rng, dims, split, smallest, largest):
    def one(position, shards_of):
        steps = jax.random.uniform(jax.random.fold_in(jax.random.fold_in(rng, 6), position), (shards_of,), jnp.float32, smallest / len(split), largest / len(split))
        return jnp.repeat(jnp.exp(steps), dims[position] // shards_of).reshape((-1,) + (1,) * (len(dims) - position - 1))

    factor_of = one(*split[0])
    for cut in split[1:]:
        factor_of = factor_of * one(*cut)
    return factor_of


def deal_out(stream_key, own, number, rows, number_of, top, limit, slope):
    sequence = jax.random.permutation(stream_key, number_of)
    crowded, common = shares(number_of, rows * top, limit, slope, True), shares(number_of, rows * top, limit, slope, False)
    places = jnp.arange(number_of)

    def named(tallies, offset_by):
        used = int((tallies > 0).sum())
        fixed = max(1, used // 4)
        shifted = fixed + (places - fixed + offset_by * (used - fixed)) % max(1, number_of - fixed)
        return jnp.zeros((number_of,), jnp.int32).at[sequence[jnp.where(places < fixed, places, shifted)]].set(jnp.asarray(tallies, jnp.int32))

    tallies = jnp.where(number % 4 == 0, named(crowded, number // 4), named(common, number - number // 4 - 1))
    mixed = jax.random.permutation(jax.random.fold_in(own, 3), number_of)
    source_of, receiver = mixed[0:number_of // 2 * 2:2], mixed[1:number_of // 2 * 2:2]
    margin = jnp.minimum(tallies[source_of] - 1, limit - tallies[receiver]) // 2
    margin = jnp.where((source_of == sequence[0]) | (receiver == sequence[0]) | (tallies[receiver] == 0), 0, jnp.maximum(margin, 0))
    shifted = jax.random.randint(jax.random.fold_in(own, 4), (number_of // 2,), 0, 1 << 20) % (margin + 1)
    tallies = tallies.at[source_of].add(-shifted).at[receiver].add(shifted)
    items = jnp.searchsorted(jnp.cumsum(tallies), jnp.arange(rows * top), side="right").astype(jnp.int32)
    table = items.reshape(top, rows).T
    table = table[jax.random.permutation(jax.random.fold_in(own, 1), rows)]
    offset_by = jax.random.randint(jax.random.fold_in(own, 2), (rows, 1), 0, top)
    return jnp.take_along_axis(table, (jnp.arange(top)[None, :] + offset_by) % top, axis=1)


def shares(number_of, total, most, slope, full):
    loads = [(1 << 20) // math.isqrt(rank ** slope) + 1 for rank in range(1, number_of + 1)]
    largest = most if full else min(most, max(-(-total // number_of), total * loads[0] // sum(loads)))
    least = 1 if total - largest >= number_of - 1 else 0
    counts, surplus = [largest] + [least] * (number_of - 1), total - largest - least * (number_of - 1)
    while surplus > 0:
        candidates = [i for i in range(1, number_of) if counts[i] < largest] or [i for i in range(1, number_of) if counts[i] < most]
        pool, budget = sum([loads[i] for i in candidates]), surplus
        for i in candidates:
            extra = min(most - counts[i], max(1, budget * loads[i] // pool), surplus)
            counts[i] = counts[i] + extra
            surplus = surplus - extra
    return np.array(counts)


def centred(rng, shape, spread, reach, cuts=(), kind=jnp.bfloat16):
    values = spread * jax.random.normal(rng, shape, jnp.float32)
    if cuts:
        values = values * levels(rng, shape, cuts, -0.22, 0.18)
    return jnp.clip(values, -reach, reach).astype(kind)


def setup_inputs(seed: int = 0) -> dict:
    splits = jax.random.split(jax.random.key(seed), 6)
    tokens = centred(splits[0], (TOKENS, D), 1.0, 6.0, ((0, 256),))
    routes_keys = jax.random.split(jax.random.fold_in(splits[1], 1), TOKENS // TOK_DEV)
    routes_turns = jax.random.permutation(jax.random.fold_in(splits[1], 3), TOKENS // TOK_DEV)
    routes = jax.vmap(lambda own, number: deal_out(jax.random.fold_in(splits[1], 2), own, number, TOK_DEV, EXPERTS, 2, CAP, 2))(routes_keys, routes_turns).reshape((TOKENS, 2))
    route_weight = jnp.clip(jnp.exp(math.log(1.0) - 2.3025851 * jax.random.uniform(splits[2], (TOKENS, 2), jnp.float32) ** levels(splits[2], (TOKENS, 2), ((0, 256),), -0.2, 0.2)), 0.1, 1.0)
    shrink_weight = centred(splits[3], (EXPERTS, R, D), D ** -0.5, 0.0625, ((0, 32),))
    expand_weight = centred(splits[4], (EXPERTS, R, D), R ** -0.5, 1.0, ((0, 32), (2, 8)))
    return dict(tokens=tokens, routes=routes, route_weight=route_weight, shrink_weight=shrink_weight, expand_weight=expand_weight)


def reference(tokens, routes, route_weight, shrink_weight, expand_weight):
    blocks = tokens.shape[0] // TOK_DEV
    shrink_float = shrink_weight.astype(jnp.float32)
    expand_float = expand_weight.astype(jnp.float32)

    def adapt_block(packed):
        block_tokens, block_routes, block_gates = packed
        flat_routes = block_routes.reshape(-1).astype(jnp.int32)
        one_hot = (flat_routes[:, None] == jnp.arange(EXPERTS, dtype=jnp.int32)[None, :]).astype(jnp.int32)
        slot_index = jnp.sum((jnp.cumsum(one_hot, axis=0) - one_hot) * one_hot, axis=1).astype(jnp.int32)
        destination = (flat_routes * CAP + slot_index).astype(jnp.int32)
        token_rows = jnp.repeat(block_tokens, 2, axis=0)
        buffer_rows = jnp.zeros((EXPERTS * CAP, D), block_tokens.dtype).at[destination].set(token_rows)
        buffer_rows = buffer_rows.reshape(EXPERTS, CAP, D)
        shrunk = jnp.einsum("ecd,erd->ecr", buffer_rows.astype(jnp.float32), shrink_float).astype(jnp.bfloat16)
        expanded = jnp.einsum("ecr,erd->ecd", shrunk.astype(jnp.float32), expand_float).astype(jnp.bfloat16)
        expanded = expanded.reshape(EXPERTS * CAP, D)
        picked = jnp.take(expanded, destination, axis=0).astype(jnp.float32).reshape(TOK_DEV, 2, D)
        mixed = picked[:, 0, :] * block_gates[:, 0:1] + picked[:, 1, :] * block_gates[:, 1:2]
        return mixed.astype(jnp.bfloat16)

    result = lax.map(adapt_block, (tokens.reshape(blocks, TOK_DEV, D), routes.reshape(blocks, TOK_DEV, 2), route_weight.reshape(blocks, TOK_DEV, 2)))
    return result.reshape(blocks * TOK_DEV, D)
```

```python
import functools

import jax
import jax.numpy as jnp
from jax import lax
from jax.experimental import pallas as pl
from jax.experimental.pallas import tpu as pltpu
from jax.sharding import PartitionSpec as P

BF16 = jnp.bfloat16
F32 = jnp.float32
ANY = pl.BlockSpec(memory_space=pl.ANY)
NT = (((1,), (1,)), ((), ()))
TN = (((0,), (0,)), ((), ()))


def params(mib=48):
    return pltpu.CompilerParams(vmem_limit_bytes=mib * 1024 * 1024)


def pack_kernel(peers, toks, rows, width, tokens_ref, weight_ref, out_ref, sems):
    copies = []
    for p in range(peers):
        cols = pl.ds(p * width, width)
        copies.append(
            pltpu.make_async_copy(tokens_ref.at[:, cols], out_ref.at[p, pl.ds(0, toks)], sems.at[0, p])
        )
        copies.append(
            pltpu.make_async_copy(weight_ref.at[:, cols], out_ref.at[p, pl.ds(toks, rows)], sems.at[1, p])
        )
    for c in copies:
        c.start()
    for c in copies:
        c.wait()


def pack(tokens, weight, peers):
    toks, d = tokens.shape
    rows = weight.shape[0]
    width = d // peers
    return pl.pallas_call(
        functools.partial(pack_kernel, peers, toks, rows, width),
        out_shape=jax.ShapeDtypeStruct((peers, toks + rows, width), tokens.dtype),
        in_specs=[ANY, ANY],
        out_specs=ANY,
        scratch_shapes=[pltpu.SemaphoreType.DMA((2, peers))],
        name="pack",
    )(tokens, weight)


def shrink_kernel(group, rank, x_ref, w_ref, r_ref, out_ref):
    peers, wrows, width = w_ref.shape
    toks = x_ref.shape[1]
    chunk = max(1, 256 // wrows)
    per = chunk * wrows // rank

    @pl.loop(0, group // 2)
    def _(g):
        x = x_ref[pl.ds(2 * g, 2)].reshape(2 * toks, width)
        routes = [[r_ref[2 * g + b, pl.ds(k, 1), :] for k in range(2)] for b in range(2)]
        acc = [[jnp.zeros((rank, toks), F32) for _ in range(2)] for _ in range(2)]
        for c in range(peers // chunk):
            w = w_ref[c * chunk : (c + 1) * chunk].reshape(chunk * wrows, width)
            p = lax.dot_general(w, x, NT, preferred_element_type=F32)
            for j in range(per):
                e = c * per + j
                for b in range(2):
                    piece = p[j * rank : (j + 1) * rank, b * toks : (b + 1) * toks]
                    for k in range(2):
                        acc[b][k] = jnp.where(routes[b][k] == e, piece, acc[b][k])
        for b in range(2):
            for k in range(2):
                out_ref[2 * g + b, pl.ds(k * rank, rank), :] = acc[b][k].astype(out_ref.dtype)


def shrink(buf, routes, toks, rank, group):
    peers, total, width = buf.shape
    wrows = total - toks
    return pl.pallas_call(
        functools.partial(shrink_kernel, group, rank),
        grid=(peers // group,),
        out_shape=jax.ShapeDtypeStruct((peers, 2 * rank, toks), F32),
        in_specs=[
            pl.BlockSpec((group, toks, width), lambda i: (i, 0, 0)),
            pl.BlockSpec((peers, wrows, width), lambda i: (0, toks // wrows, 0)),
            pl.BlockSpec((group, 2, toks), lambda i: (i, 0, 0)),
        ],
        out_specs=pl.BlockSpec((group, 2 * rank, toks), lambda i: (i, 0, 0)),
        compiler_params=params(),
        name="shrink",
    )(buf, buf, routes)


def combine_kernel(peers, per_block, rank, toks, part_ref, gate_ref, weight_ref, out_ref, s_ref, sems):
    wrows = weight_ref.shape[1]
    width = out_ref.shape[2]
    copies = []
    for p in range(peers):
        z, q = p // per_block, p % per_block
        copies.append(
            pltpu.make_async_copy(
                weight_ref.at[z, :, pl.ds(q * width, width)], out_ref.at[p, pl.ds(0, wrows)], sems.at[0, p]
            )
        )
    for c in copies:
        c.start()
    for k in range(2):
        total = jnp.sum(part_ref[:, pl.ds(k * rank, rank), :], axis=0)
        gated = total.astype(BF16).astype(F32) * gate_ref[pl.ds(k, 1), :]
        s_ref[:, pl.ds(k * toks, toks)] = gated.astype(BF16)
    sends = []
    for p in range(peers):
        sends.append(pltpu.make_async_copy(s_ref, out_ref.at[p, pl.ds(wrows, rank)], sems.at[1, p]))
    for c in sends:
        c.start()
    for c in copies + sends:
        c.wait()


def combine(part, gates, weight):
    peers, rank2, toks = part.shape
    rank = rank2 // 2
    blocks, wrows, cols = weight.shape
    per_block = peers // blocks
    width = cols // per_block
    return pl.pallas_call(
        functools.partial(combine_kernel, peers, per_block, rank, toks),
        out_shape=jax.ShapeDtypeStruct((peers, wrows + rank, width), BF16),
        in_specs=[pl.BlockSpec(memory_space=pltpu.VMEM), pl.BlockSpec(memory_space=pltpu.VMEM), ANY],
        out_specs=ANY,
        scratch_shapes=[pltpu.VMEM((rank, 2 * toks), BF16), pltpu.SemaphoreType.DMA((2, peers))],
        compiler_params=params(),
        name="combine",
    )(part, gates, weight)


def expand_kernel(group, s_ref, w_ref, r_ref, out_ref, a_ref):
    peers, wrows, width = w_ref.shape
    rank = s_ref.shape[1]
    toks = s_ref.shape[2] // 2
    lanes = 128
    per = lanes // rank
    tiles = peers * wrows // lanes
    src = lax.broadcasted_iota(jnp.int32, (4 * rank, 4 * lanes), 0)
    dst = lax.broadcasted_iota(jnp.int32, (4 * rank, 4 * lanes), 1)
    spread = (src == (dst // lanes) * rank + dst % rank).astype(F32).astype(BF16)
    lane_expert = (lax.broadcasted_iota(jnp.int32, (toks, lanes), 1) // rank).astype(F32)
    zero = jnp.zeros((toks, lanes), BF16)

    @pl.loop(0, group)
    def _(b):
        s = s_ref[b].astype(F32)
        r = r_ref[b].astype(F32)
        rows = jnp.concatenate(
            [s[:, :toks], s[:, toks:]] + [jnp.broadcast_to(r[k : k + 1], (rank, toks)) for k in range(2)], axis=0
        ).astype(BF16)
        t = lax.dot_general(rows, spread, TN, preferred_element_type=F32)
        s0 = t[:, :lanes].astype(BF16)
        s1 = t[:, lanes : 2 * lanes].astype(BF16)
        d0 = (t[:, 2 * lanes : 3 * lanes] - lane_expert).astype(BF16)
        d1 = (t[:, 3 * lanes :] - lane_expert).astype(BF16)
        for j in range(tiles):
            e = jnp.asarray(j * per, BF16)
            a = jnp.where(d0 == e, s0, jnp.where(d1 == e, s1, zero))
            a_ref[pl.ds(pl.multiple_of(b * toks, toks), toks), j * lanes : (j + 1) * lanes] = a

    w = w_ref[...].reshape(peers * wrows, width)
    out = jnp.dot(a_ref[...], w, preferred_element_type=F32)
    out_ref[...] = out.astype(BF16).reshape(group, toks, width)


def expand(buf, routes, rank, group):
    peers, total, width = buf.shape
    wrows = total - rank
    toks = routes.shape[2]
    return pl.pallas_call(
        functools.partial(expand_kernel, group),
        grid=(peers // group,),
        out_shape=jax.ShapeDtypeStruct((peers, toks, width), BF16),
        in_specs=[
            pl.BlockSpec((group, rank, width), lambda i: (i, wrows // rank, 0)),
            pl.BlockSpec((peers, wrows, width), lambda i: (0, 0, 0)),
            pl.BlockSpec((group, 2, toks), lambda i: (i, 0, 0)),
        ],
        out_specs=pl.BlockSpec((group, toks, width), lambda i: (i, 0, 0)),
        scratch_shapes=[pltpu.VMEM((group * toks, peers * wrows), BF16)],
        compiler_params=params(),
        name="expand",
    )(buf, buf, routes)


def unpack_kernel(peers, width, in_ref, out_ref, sems):
    copies = [
        pltpu.make_async_copy(in_ref.at[p], out_ref.at[:, pl.ds(p * width, width)], sems.at[p]) for p in range(peers)
    ]
    for c in copies:
        c.start()
    for c in copies:
        c.wait()


def unpack(buf):
    peers, toks, width = buf.shape
    return pl.pallas_call(
        functools.partial(unpack_kernel, peers, width),
        out_shape=jax.ShapeDtypeStruct((toks, peers * width), buf.dtype),
        in_specs=[ANY],
        out_specs=ANY,
        scratch_shapes=[pltpu.SemaphoreType.DMA((peers,))],
        name="unpack",
    )(buf)


def swap(x):
    return lax.all_to_all(x, "expert", split_axis=0, concat_axis=0, tiled=True)


def per_device(tokens, routes, route_weight, shrink_weight, expand_weight):
    toks, _ = tokens.shape
    local, rank, _ = shrink_weight.shape
    peers = lax.axis_size("expert")
    rows = local * rank
    group = min(8, peers)
    all_routes = lax.all_gather(routes.T, "expert", axis=0)
    all_expand = lax.all_gather(expand_weight.reshape(rows, -1), "tensor", axis=0)
    arrived = swap(pack(tokens, shrink_weight.reshape(rows, -1), peers))
    partial = shrink(arrived, all_routes, toks, rank, group)
    packed = swap(combine(swap(partial), route_weight.T, all_expand))
    columns = expand(packed, all_routes, rank, group)
    return unpack(swap(columns))


def solution(mesh):
    return jax.shard_map(
        per_device,
        mesh=mesh,
        in_specs=(
            P(("expert", "tensor"), None),
            P(("expert", "tensor"), None),
            P(("expert", "tensor"), None),
            P("expert", None, None),
            P("expert", None, "tensor"),
        ),
        out_specs=P(("expert", "tensor"), None),
        check_vma=False,
    )
```

```python
import functools

import jax
import jax.numpy as jnp
from jax import lax
from jax.experimental import pallas as pl
from jax.experimental.pallas import tpu as pltpu
from jax.sharding import PartitionSpec as P

BF16 = jnp.bfloat16
F32 = jnp.float32
ANY = pl.BlockSpec(memory_space=pl.ANY)
VM = pl.BlockSpec(memory_space=pltpu.VMEM)
NT = (((1,), (1,)), ((), ()))
TN = (((0,), (0,)), ((), ()))


def params(mib=48):
    return pltpu.CompilerParams(vmem_limit_bytes=mib * 1024 * 1024)


def pack_kernel(peers, toks, rows, width, tokens_ref, weight_ref, routes_ref, out_ref, sems):
    copies = []
    for p in range(peers):
        cols = pl.ds(p * width, width)
        copies.append(
            pltpu.make_async_copy(tokens_ref.at[:, cols], out_ref.at[p, pl.ds(0, toks)], sems.at[0, p])
        )
        copies.append(
            pltpu.make_async_copy(weight_ref.at[:, cols], out_ref.at[p, pl.ds(toks, rows)], sems.at[1, p])
        )
    for c in copies:
        c.start()
    for p in range(peers):
        out_ref[p, pl.ds(toks + rows, 16), :] = routes_ref[...]
    for c in copies:
        c.wait()


def pack(tokens, weight, routes, peers):
    toks, d = tokens.shape
    rows = weight.shape[0]
    width = d // peers
    return pl.pallas_call(
        functools.partial(pack_kernel, peers, toks, rows, width),
        out_shape=jax.ShapeDtypeStruct((peers, toks + rows + 16, width), tokens.dtype),
        in_specs=[ANY, ANY, VM],
        out_specs=VM,
        scratch_shapes=[pltpu.SemaphoreType.DMA((2, peers))],
        compiler_params=params(16),
        name="pack",
    )(tokens, weight, routes)


def shrink_kernel(group, rank, x_ref, w_ref, r_ref, out_ref):
    peers, wrows, width = w_ref.shape
    toks = x_ref.shape[1]
    chunk = max(1, 256 // wrows)
    per = chunk * wrows // rank

    @pl.loop(0, group // 2)
    def _(g):
        x = x_ref[pl.ds(2 * g, 2)].reshape(2 * toks, width)
        rows = [r_ref[2 * g + b].astype(F32)[0:1] for b in range(2)]
        routes = [[r[:, :toks], r[:, toks:]] for r in rows]
        acc = [[jnp.zeros((rank, toks), F32) for _ in range(2)] for _ in range(2)]
        for c in range(peers // chunk):
            w = w_ref[c * chunk : (c + 1) * chunk].reshape(chunk * wrows, width)
            p = lax.dot_general(w, x, NT, preferred_element_type=F32)
            for j in range(per):
                e = c * per + j
                for b in range(2):
                    piece = p[j * rank : (j + 1) * rank, b * toks : (b + 1) * toks]
                    for k in range(2):
                        acc[b][k] = jnp.where(routes[b][k] == e, piece, acc[b][k])
        for b in range(2):
            for k in range(2):
                out_ref[2 * g + b, pl.ds(k * rank, rank), :] = acc[b][k].astype(out_ref.dtype)


def shrink(buf, toks, rank, group):
    peers, total, width = buf.shape
    wrows = total - toks - 16
    return pl.pallas_call(
        functools.partial(shrink_kernel, group, rank),
        grid=(peers // group,),
        out_shape=jax.ShapeDtypeStruct((peers, 2 * rank, toks), F32),
        in_specs=[
            pl.BlockSpec((group, toks, width), lambda i: (i, 0, 0)),
            pl.BlockSpec((peers, wrows, width), lambda i: (0, toks // wrows, 0)),
            pl.BlockSpec((group, 16, width), lambda i: (i, (toks + wrows) // 16, 0)),
        ],
        out_specs=pl.BlockSpec((group, 2 * rank, toks), lambda i: (i, 0, 0)),
        compiler_params=params(),
        name="shrink",
    )(buf, buf, buf)


def combine_kernel(peers, per_block, rank, toks, part_ref, gate_ref, weight_ref, out_ref, s_ref, sems):
    wrows = weight_ref.shape[1]
    width = out_ref.shape[2]
    copies = []
    for p in range(peers):
        z, q = p // per_block, p % per_block
        copies.append(
            pltpu.make_async_copy(
                weight_ref.at[z, :, pl.ds(q * width, width)], out_ref.at[p, pl.ds(0, wrows)], sems.at[0, p]
            )
        )
    for c in copies:
        c.start()
    for k in range(2):
        total = jnp.sum(part_ref[:, pl.ds(k * rank, rank), :], axis=0)
        gated = total.astype(BF16).astype(F32) * gate_ref[pl.ds(k, 1), :]
        s_ref[:, pl.ds(k * toks, toks)] = gated.astype(BF16)
    sends = []
    for p in range(peers):
        sends.append(pltpu.make_async_copy(s_ref, out_ref.at[p, pl.ds(wrows, rank)], sems.at[1, p]))
    for c in sends:
        c.start()
    for c in copies + sends:
        c.wait()


def combine(part, gates, weight):
    peers, rank2, toks = part.shape
    rank = rank2 // 2
    blocks, wrows, cols = weight.shape
    per_block = peers // blocks
    width = cols // per_block
    return pl.pallas_call(
        functools.partial(combine_kernel, peers, per_block, rank, toks),
        out_shape=jax.ShapeDtypeStruct((peers, wrows + rank, width), BF16),
        in_specs=[VM, VM, ANY],
        out_specs=ANY,
        scratch_shapes=[pltpu.VMEM((rank, 2 * toks), BF16), pltpu.SemaphoreType.DMA((2, peers))],
        compiler_params=params(),
        name="combine",
    )(part, gates, weight)


def expand_kernel(group, s_ref, w_ref, r_ref, out_ref, a_ref):
    peers, wrows, width = w_ref.shape
    rank = s_ref.shape[1]
    toks = s_ref.shape[2] // 2
    lanes = 128
    per = lanes // rank
    tiles = peers * wrows // lanes
    src = lax.broadcasted_iota(jnp.int32, (4 * rank, 4 * lanes), 0)
    dst = lax.broadcasted_iota(jnp.int32, (4 * rank, 4 * lanes), 1)
    spread = (src == (dst // lanes) * rank + dst % rank).astype(F32).astype(BF16)
    lane_expert = (lax.broadcasted_iota(jnp.int32, (toks, lanes), 1) // rank).astype(F32)
    zero = jnp.zeros((toks, lanes), BF16)

    @pl.loop(0, group)
    def _(b):
        s = s_ref[b].astype(F32)
        r = r_ref[b].astype(F32)[0:1]
        rows = jnp.concatenate(
            [s[:, :toks], s[:, toks:]] + [jnp.broadcast_to(t, (rank, toks)) for t in (r[:, :toks], r[:, toks:])], axis=0
        ).astype(BF16)
        t = lax.dot_general(rows, spread, TN, preferred_element_type=F32)
        s0 = t[:, :lanes].astype(BF16)
        s1 = t[:, lanes : 2 * lanes].astype(BF16)
        d0 = (t[:, 2 * lanes : 3 * lanes] - lane_expert).astype(BF16)
        d1 = (t[:, 3 * lanes :] - lane_expert).astype(BF16)
        for j in range(tiles):
            e = jnp.asarray(j * per, BF16)
            a = jnp.where(d0 == e, s0, jnp.where(d1 == e, s1, zero))
            a_ref[pl.ds(pl.multiple_of(b * toks, toks), toks), j * lanes : (j + 1) * lanes] = a

    w = w_ref[...].reshape(peers * wrows, width)
    out = jnp.dot(a_ref[...], w, preferred_element_type=F32)
    out_ref[...] = out.astype(BF16).reshape(group, toks, width)


def expand(buf, arrived, rank, group):
    peers, total, width = buf.shape
    wrows = total - rank
    toks = width // 2
    route_block = arrived.shape[1] // 16 - 1
    return pl.pallas_call(
        functools.partial(expand_kernel, group),
        grid=(peers // group,),
        out_shape=jax.ShapeDtypeStruct((peers, toks, width), BF16),
        in_specs=[
            pl.BlockSpec((group, rank, width), lambda i: (i, wrows // rank, 0)),
            pl.BlockSpec((peers, wrows, width), lambda i: (0, 0, 0)),
            pl.BlockSpec((group, 16, width), lambda i: (i, route_block, 0)),
        ],
        out_specs=pl.BlockSpec((group, toks, width), lambda i: (i, 0, 0)),
        scratch_shapes=[pltpu.VMEM((group * toks, peers * wrows), BF16)],
        compiler_params=params(),
        name="expand",
    )(buf, buf, arrived)


def unpack_kernel(peers, width, in_ref, out_ref, sems):
    copies = [
        pltpu.make_async_copy(in_ref.at[p], out_ref.at[:, pl.ds(p * width, width)], sems.at[p]) for p in range(peers)
    ]
    for c in copies:
        c.start()
    for c in copies:
        c.wait()


def unpack(buf):
    peers, toks, width = buf.shape
    return pl.pallas_call(
        functools.partial(unpack_kernel, peers, width),
        out_shape=jax.ShapeDtypeStruct((toks, peers * width), buf.dtype),
        in_specs=[VM],
        out_specs=ANY,
        scratch_shapes=[pltpu.SemaphoreType.DMA((peers,))],
        compiler_params=params(16),
        name="unpack",
    )(buf)


def swap(x):
    return lax.all_to_all(x, "expert", split_axis=0, concat_axis=0, tiled=True)


def per_device(tokens, routes, route_weight, shrink_weight, expand_weight):
    toks, _ = tokens.shape
    local, rank, _ = shrink_weight.shape
    peers = lax.axis_size("expert")
    rows = local * rank
    group = min(8, peers)
    route_rows = jnp.broadcast_to(routes.T.astype(BF16).reshape(1, 2 * toks), (16, 2 * toks))
    all_expand = lax.all_gather(expand_weight.reshape(rows, -1), "tensor", axis=0)
    arrived = swap(pack(tokens, shrink_weight.reshape(rows, -1), route_rows, peers))
    partial = shrink(arrived, toks, rank, group)
    packed = swap(combine(swap(partial), route_weight.T, all_expand))
    columns = expand(packed, arrived, rank, group)
    return unpack(swap(columns))


def solution(mesh):
    return jax.shard_map(
        per_device,
        mesh=mesh,
        in_specs=(
            P(("expert", "tensor"), None),
            P(("expert", "tensor"), None),
            P(("expert", "tensor"), None),
            P("expert", None, None),
            P("expert", None, "tensor"),
        ),
        out_specs=P(("expert", "tensor"), None),
        check_vma=False,
    )
```

```python
import functools

import jax
import jax.numpy as jnp
from jax import lax
from jax.experimental import pallas as pl
from jax.experimental.pallas import tpu as pltpu
from jax.sharding import PartitionSpec as P

BF16 = jnp.bfloat16
F32 = jnp.float32
ANY = pl.BlockSpec(memory_space=pl.ANY)
HBM = pl.BlockSpec(memory_space=pltpu.HBM)
VM = pl.BlockSpec(memory_space=pltpu.VMEM)
NT = (((1,), (1,)), ((), ()))
TILE = 16
LANES = 128


def params(mib):
    return pltpu.CompilerParams(vmem_limit_bytes=mib * 1024 * 1024)


def pack_kernel(peers, toks, rows, width, tokens_ref, weight_ref, expand_ref, routes_ref, out_ref, sems):
    copies = []
    for p in range(peers):
        cols = pl.ds(p * width, width)
        copies.append(
            pltpu.make_async_copy(tokens_ref.at[:, cols], out_ref.at[p, pl.ds(0, toks)], sems.at[0, p])
        )
        copies.append(
            pltpu.make_async_copy(weight_ref.at[:, cols], out_ref.at[p, pl.ds(toks, rows)], sems.at[1, p])
        )
    for c in copies:
        c.start()
    tail = pl.ds(toks + rows, TILE)
    names = routes_ref[...].astype(F32)
    names = jnp.concatenate([names, jnp.zeros((TILE - 2, toks), F32)], axis=0).astype(BF16)
    feats = expand_ref.shape[1] // peers
    for t in range(expand_ref.shape[1] // LANES):
        block = expand_ref[:, t * LANES : (t + 1) * LANES].astype(F32).T
        for j in range(LANES // feats):
            p = t * (LANES // feats) + j
            piece = block[j * feats : (j + 1) * feats]
            piece = jnp.concatenate([piece[:TILE], piece[TILE:]], axis=1)
            out_ref[p, tail, pl.ds(0, LANES)] = piece.astype(BF16)
            out_ref[p, tail, pl.ds(LANES, toks)] = names
    for c in copies:
        c.wait()


def pack(tokens, weight, expand_weight, routes, peers):
    toks, d = tokens.shape
    rows = weight.shape[0]
    width = d // peers
    return pl.pallas_call(
        functools.partial(pack_kernel, peers, toks, rows, width),
        out_shape=jax.ShapeDtypeStruct((peers, toks + rows + TILE, width), tokens.dtype),
        in_specs=[HBM, HBM, VM, VM],
        out_specs=VM,
        scratch_shapes=[pltpu.SemaphoreType.DMA((2, peers))],
        compiler_params=params(16),
        name="pack",
    )(tokens, weight, expand_weight, routes)


def shrink_kernel(group, rank, x_ref, w_ref, r_ref, out_ref):
    peers, wrows, width = w_ref.shape
    toks = x_ref.shape[1]
    chunk = max(1, 256 // wrows)
    per = chunk * wrows // rank
    x = x_ref[...].reshape(group * toks, width)
    names = [r_ref[b].astype(F32) for b in range(group)]
    acc = [[jnp.zeros((rank, toks), F32) for _ in range(2)] for _ in range(group)]
    for c in range(peers // chunk):
        w = w_ref[c * chunk : (c + 1) * chunk].reshape(chunk * wrows, width)
        p = lax.dot_general(w, x, NT, preferred_element_type=F32)
        for j in range(per):
            e = c * per + j
            for b in range(group):
                piece = p[j * rank : (j + 1) * rank, b * toks : (b + 1) * toks]
                for k in range(2):
                    acc[b][k] = jnp.where(names[b][k : k + 1] == e, piece, acc[b][k])
    for b in range(group):
        for k in range(2):
            out_ref[b, pl.ds(k * rank, rank), :] = acc[b][k].astype(out_ref.dtype)


def shrink(buf, toks, rows, rank, group):
    peers, _, width = buf.shape
    tail = (toks + rows) // TILE
    return pl.pallas_call(
        functools.partial(shrink_kernel, group, rank),
        grid=(peers // group,),
        out_shape=jax.ShapeDtypeStruct((peers, 2 * rank, toks), BF16),
        in_specs=[
            pl.BlockSpec((group, toks, width), lambda i: (i, 0, 0)),
            pl.BlockSpec((peers, rows, width), lambda i: (0, toks // rows, 0)),
            pl.BlockSpec((group, TILE, LANES), lambda i: (i, tail, 1)),
        ],
        out_specs=pl.BlockSpec((group, 2 * rank, toks), lambda i: (i, 0, 0)),
        compiler_params=params(32),
        name="shrink",
    )(buf, buf, buf)


def combine_kernel(peers, rank, part_ref, gate_ref, out_ref):
    gated = []
    for k in range(2):
        total = part_ref[0, pl.ds(k * rank, rank), :].astype(F32)
        for p in range(1, peers):
            total = total + part_ref[p, pl.ds(k * rank, rank), :].astype(F32)
        gated.append((total.astype(BF16).astype(F32) * gate_ref[pl.ds(k, 1), :]).astype(BF16))
    both = jnp.concatenate(gated, axis=1)
    for p in range(peers):
        out_ref[p] = both


def combine(part, gates):
    peers, rank2, toks = part.shape
    rank = rank2 // 2
    return pl.pallas_call(
        functools.partial(combine_kernel, peers, rank),
        out_shape=jax.ShapeDtypeStruct((peers, rank, 2 * toks), BF16),
        in_specs=[VM, VM],
        out_specs=VM,
        compiler_params=params(16),
        name="combine",
    )(part, gates)


def expand_kernel(group, experts, order, s_ref, r_ref, *refs):
    *piece_refs, out_ref, w_ref = refs
    rank = s_ref.shape[1]
    toks = s_ref.shape[2] // 2

    @pl.when(pl.program_id(0) == 0)
    def _():
        me = lax.axis_index("tensor")
        low = lax.broadcasted_iota(jnp.int32, (TILE, LANES), 1) < LANES // 2
        blocks = []
        for ref in piece_refs:
            blocks += [ref.at[m] for m in range(ref.shape[0])]
        for offset, ref in zip(order, blocks):
            row = pl.multiple_of((me ^ offset) * (2 * TILE), 2 * TILE)
            for t in range(ref.shape[0] // 2):
                a = ref[2 * t].astype(F32)
                b = ref[2 * t + 1].astype(F32)
                first = jnp.where(low, a, pltpu.roll(b, LANES // 2, 1))
                second = jnp.where(low, pltpu.roll(a, LANES // 2, 1), b)
                both = jnp.concatenate([first, second], axis=0).astype(BF16)
                w_ref[pl.ds(row, 2 * TILE), t * LANES : (t + 1) * LANES] = both

    spread = []
    for b in range(group):
        s = s_ref[b]
        names = r_ref[b]
        s0, s1 = s[:, :toks], s[:, toks:]
        r0, r1 = (jnp.broadcast_to(names[k : k + 1], (rank, toks)) for k in range(2))
        zero = jnp.zeros((rank, toks), BF16)
        rows = []
        for e in range(experts):
            name = jnp.asarray(e, BF16)
            rows.append(jnp.where(r0 == name, s0, jnp.where(r1 == name, s1, zero)))
        spread.append(jnp.concatenate(rows, axis=0))
    out = jnp.dot(w_ref[...], jnp.concatenate(spread, axis=1), preferred_element_type=F32)
    for b in range(group):
        out_ref[b] = out[:, b * toks : (b + 1) * toks].astype(BF16)


def expand(vectors, arrived, pieces, order, experts, group):
    peers, rank, toks2 = vectors.shape
    toks = toks2 // 2
    tail = arrived.shape[1] // TILE - 1
    feats = len(order) * 2 * TILE
    return pl.pallas_call(
        functools.partial(expand_kernel, group, experts, order),
        grid=(peers // group,),
        out_shape=jax.ShapeDtypeStruct((peers, feats, toks), BF16),
        in_specs=[
            pl.BlockSpec((group, rank, toks2), lambda i: (i, 0, 0)),
            pl.BlockSpec((group, TILE, LANES), lambda i: (i, tail, 1)),
        ]
        + [pl.BlockSpec(p.shape, lambda i: (0, 0, 0, 0)) for p in pieces],
        out_specs=pl.BlockSpec((group, feats, toks), lambda i: (i, 0, 0)),
        scratch_shapes=[pltpu.VMEM((feats, experts * rank), BF16)],
        compiler_params=params(32),
        name="expand",
    )(vectors, arrived, *pieces)


def unpack_kernel(blocks, in_ref, out_ref, buf, sems):
    peers, feats, toks = in_ref.shape
    piece = feats // blocks
    per = LANES // piece
    cols = peers * piece
    copies = []
    for z in range(blocks):
        for q in range(peers // per):
            parts = [in_ref[per * q + k, z * piece : (z + 1) * piece, :] for k in range(per)]
            buf[z, q] = jnp.concatenate(parts, axis=0).T
            copy = pltpu.make_async_copy(
                buf.at[z, q], out_ref.at[:, pl.ds(z * cols + q * LANES, LANES)], sems.at[z, q]
            )
            copy.start()
            copies.append(copy)
    for copy in copies:
        copy.wait()


def unpack(buf, blocks):
    peers, feats, toks = buf.shape
    quads = peers * (feats // blocks) // LANES
    return pl.pallas_call(
        functools.partial(unpack_kernel, blocks),
        out_shape=jax.ShapeDtypeStruct((toks, peers * feats), buf.dtype),
        in_specs=[VM],
        out_specs=ANY,
        scratch_shapes=[
            pltpu.VMEM((blocks, quads, toks, LANES), buf.dtype),
            pltpu.SemaphoreType.DMA((blocks, quads)),
        ],
        compiler_params=params(16),
        name="unpack",
    )(buf)


def swap(x):
    return lax.all_to_all(x, "expert", split_axis=0, concat_axis=0, tiled=True)


def across(x, blocks, offset):
    return lax.ppermute(x, "tensor", [(i, i ^ offset) for i in range(blocks)])


def per_device(tokens, routes, route_weight, shrink_weight, expand_weight):
    toks, _ = tokens.shape
    local, rank, _ = shrink_weight.shape
    peers = lax.axis_size("expert")
    blocks = lax.axis_size("tensor")
    rows = local * rank
    group = min(8, peers)
    arrived = swap(
        pack(tokens, shrink_weight.reshape(rows, -1), expand_weight.reshape(rows, -1), routes.T, peers)
    )
    pieces = [arrived[None, :, toks + rows :, :LANES]]
    order = [0]
    offset = blocks // 2
    while offset:
        held = pieces[0] if len(pieces) == 1 else jnp.concatenate(pieces, axis=0)
        pieces.append(across(held, blocks, offset))
        order += [o ^ offset for o in order]
        offset //= 2
    partial = shrink(arrived, toks, rows, rank, group)
    vectors = swap(combine(swap(partial), route_weight.T))
    columns = expand(vectors, arrived, pieces, tuple(order), peers * local, group)
    return unpack(swap(columns), blocks)


def solution(mesh):
    return jax.shard_map(
        per_device,
        mesh=mesh,
        in_specs=(
            P(("expert", "tensor"), None),
            P(("expert", "tensor"), None),
            P(("expert", "tensor"), None),
            P("expert", None, None),
            P("expert", None, "tensor"),
        ),
        out_specs=P(("expert", "tensor"), None),
        check_vma=False,
    )
```

```python
import functools

import jax
import jax.numpy as jnp
from jax import lax
from jax.experimental import pallas as pl
from jax.experimental.pallas import tpu as pltpu
from jax.sharding import PartitionSpec as P

BF16 = jnp.bfloat16
F32 = jnp.float32
ANY = pl.BlockSpec(memory_space=pl.ANY)
HBM = pl.BlockSpec(memory_space=pltpu.HBM)
VM = pl.BlockSpec(memory_space=pltpu.VMEM)
NT = (((1,), (1,)), ((), ()))
TILE = 16
LANES = 128


def params(mib):
    return pltpu.CompilerParams(vmem_limit_bytes=mib * 1024 * 1024)


def pack_kernel(peers, toks, rows, width, tokens_ref, weight_ref, routes_ref, out_ref, buf, sems):
    copies = []
    for p in range(peers):
        cols = pl.ds(p * width, width)
        first = pltpu.make_async_copy(tokens_ref.at[:, cols], buf.at[p, pl.ds(0, toks)], sems.at[0, p])
        second = pltpu.make_async_copy(weight_ref.at[:, cols], buf.at[p, pl.ds(toks, rows)], sems.at[1, p])
        first.start()
        second.start()
        copies.append((first, second))
    names = jnp.broadcast_to(routes_ref[pl.ds(0, 1), :], (TILE, width)).astype(F32).astype(BF16)
    for p in range(peers):
        buf[p, pl.ds(toks + rows, TILE), :] = names
    sends = []
    for p in range(peers):
        for copy in copies[p]:
            copy.wait()
        send = pltpu.make_async_copy(buf.at[p], out_ref.at[p], sems.at[2, p])
        send.start()
        sends.append(send)
    for send in sends:
        send.wait()


def pack(tokens, weight, routes, peers):
    toks, d = tokens.shape
    rows = weight.shape[0]
    width = d // peers
    shape = (peers, toks + rows + TILE, width)
    return pl.pallas_call(
        functools.partial(pack_kernel, peers, toks, rows, width),
        out_shape=jax.ShapeDtypeStruct(shape, tokens.dtype),
        in_specs=[HBM, HBM, VM],
        out_specs=HBM,
        scratch_shapes=[pltpu.VMEM(shape, tokens.dtype), pltpu.SemaphoreType.DMA((3, peers))],
        compiler_params=params(56),
        name="pack",
    )(tokens, weight, routes)


def shrink_kernel(group, rank, x_ref, w_ref, r_ref, out_ref):
    peers, wrows, width = w_ref.shape
    toks = x_ref.shape[1]
    chunk = max(1, 256 // wrows)
    per = chunk * wrows // rank
    x = x_ref[...].reshape(group * toks, width)
    names = [r_ref[b].astype(F32)[0:1] for b in range(group)]
    acc = [[jnp.zeros((rank, toks), F32) for _ in range(2)] for _ in range(group)]
    for c in range(peers // chunk):
        w = w_ref[c * chunk : (c + 1) * chunk].reshape(chunk * wrows, width)
        p = lax.dot_general(w, x, NT, preferred_element_type=F32)
        for j in range(per):
            e = c * per + j
            for b in range(group):
                piece = p[j * rank : (j + 1) * rank, b * toks : (b + 1) * toks]
                for k in range(2):
                    acc[b][k] = jnp.where(names[b][:, k * toks : (k + 1) * toks] == e, piece, acc[b][k])
    for b in range(group):
        for k in range(2):
            out_ref[b, pl.ds(k * rank, rank), :] = acc[b][k].astype(out_ref.dtype)


def shrink(buf, toks, rows, rank, group):
    peers, _, width = buf.shape
    tail = (toks + rows) // TILE
    return pl.pallas_call(
        functools.partial(shrink_kernel, group, rank),
        grid=(peers // group,),
        out_shape=jax.ShapeDtypeStruct((peers, 2 * rank, toks), BF16),
        in_specs=[
            pl.BlockSpec((group, toks, width), lambda i: (i, 0, 0)),
            pl.BlockSpec((peers, rows, width), lambda i: (0, toks // rows, 0)),
            pl.BlockSpec((group, TILE, width), lambda i: (i, tail, 0)),
        ],
        out_specs=pl.BlockSpec((group, 2 * rank, toks), lambda i: (i, 0, 0)),
        compiler_params=params(32),
        name="shrink",
    )(buf, buf, buf)


def place_kernel(blocks, width, *refs):
    *block_refs, out_ref, sems = refs
    rows = block_refs[0].shape[0]
    per = block_refs[0].shape[1] // width
    me = lax.axis_index("tensor")
    copies = []
    for offset, ref in enumerate(block_refs):
        owner = lax.rem(me + offset, blocks)
        for q in range(per):
            copy = pltpu.make_async_copy(
                ref.at[:, pl.ds(q * width, width)], out_ref.at[owner * per + q, pl.ds(0, rows)], sems.at[offset, q]
            )
            copy.start()
            copies.append(copy)
    for copy in copies:
        copy.wait()


def place(held, peers, rank):
    blocks = len(held)
    rows, cols = held[0].shape
    width = blocks * cols // peers
    return pl.pallas_call(
        functools.partial(place_kernel, blocks, width),
        out_shape=jax.ShapeDtypeStruct((peers, rows + rank, width), BF16),
        in_specs=[VM] * blocks,
        out_specs=VM,
        scratch_shapes=[pltpu.SemaphoreType.DMA((blocks, peers // blocks))],
        compiler_params=params(16),
        name="place",
    )(*held)


def combine_kernel(peers, rank, part_ref, gate_ref, _, out_ref, both_ref, sems):
    rows = out_ref.shape[1] - rank
    toks = part_ref.shape[2]
    for k in range(2):
        total = part_ref[0, pl.ds(k * rank, rank), :].astype(F32)
        for p in range(1, peers):
            total = total + part_ref[p, pl.ds(k * rank, rank), :].astype(F32)
        gated = total.astype(BF16).astype(F32) * gate_ref[pl.ds(k, 1), :]
        both_ref[:, k * toks : (k + 1) * toks] = gated.astype(BF16)
    copies = [pltpu.make_async_copy(both_ref, out_ref.at[p, pl.ds(rows, rank)], sems.at[p]) for p in range(peers)]
    for copy in copies:
        copy.start()
    for copy in copies:
        copy.wait()


def combine(part, gates, placed):
    peers, rank2, toks = part.shape
    return pl.pallas_call(
        functools.partial(combine_kernel, peers, rank2 // 2),
        out_shape=jax.ShapeDtypeStruct(placed.shape, BF16),
        in_specs=[VM, VM, ANY],
        out_specs=ANY,
        scratch_shapes=[pltpu.VMEM((rank2 // 2, 2 * toks), BF16), pltpu.SemaphoreType.DMA((peers,))],
        input_output_aliases={2: 0},
        compiler_params=params(16),
        name="combine",
    )(part, gates, placed)


def expand_kernel(group, rank, s_ref, r_ref, w_ref, out_ref, t_ref):
    toks = s_ref.shape[2] // 2
    peers, rows, _ = w_ref.shape
    experts = peers * rows // rank
    per = LANES // rows

    @pl.when(pl.program_id(0) == 0)
    def _():
        for t in range(peers // per):
            block = jnp.concatenate([w_ref[t * per + j] for j in range(per)], axis=0)
            t_ref[:, t * LANES : (t + 1) * LANES] = block.T

    spread = []
    for b in range(group):
        s = s_ref[b]
        names = r_ref[b]
        s0, s1 = s[:, :toks], s[:, toks:]
        r0, r1 = (jnp.broadcast_to(names[:1, k * toks : (k + 1) * toks], (rank, toks)) for k in range(2))
        zero = jnp.zeros((rank, toks), BF16)
        pieces = []
        for e in range(experts):
            name = jnp.asarray(e, BF16)
            pieces.append(jnp.where(r0 == name, s0, jnp.where(r1 == name, s1, zero)))
        spread.append(jnp.concatenate(pieces, axis=0))
    out = jnp.dot(t_ref[...], jnp.concatenate(spread, axis=1), preferred_element_type=F32)
    for b in range(group):
        out_ref[b] = out[:, b * toks : (b + 1) * toks].astype(BF16)


def expand(vectors, arrived, rank, group):
    peers, total, width = vectors.shape
    rows = total - rank
    toks = width // 2
    tail = arrived.shape[1] // TILE - 1
    return pl.pallas_call(
        functools.partial(expand_kernel, group, rank),
        grid=(peers // group,),
        out_shape=jax.ShapeDtypeStruct((peers, width, toks), BF16),
        in_specs=[
            pl.BlockSpec((group, rank, width), lambda i: (i, rows // rank, 0)),
            pl.BlockSpec((group, TILE, width), lambda i: (i, tail, 0)),
            pl.BlockSpec((peers, rows, width), lambda i: (0, 0, 0)),
        ],
        out_specs=pl.BlockSpec((group, width, toks), lambda i: (i, 0, 0)),
        scratch_shapes=[pltpu.VMEM((width, peers * rows), BF16)],
        compiler_params=params(32),
        name="expand",
    )(vectors, arrived, vectors)


def unpack_kernel(in_ref, out_ref, buf, sems):
    peers, width, _ = in_ref.shape
    copies = []
    for p in range(peers):
        for q in range(width // LANES):
            buf[p, :, q * LANES : (q + 1) * LANES] = in_ref[p, q * LANES : (q + 1) * LANES, :].T
        copy = pltpu.make_async_copy(buf.at[p], out_ref.at[:, pl.ds(p * width, width)], sems.at[p])
        copy.start()
        copies.append(copy)
    for copy in copies:
        copy.wait()


def unpack(buf):
    peers, width, toks = buf.shape
    return pl.pallas_call(
        unpack_kernel,
        out_shape=jax.ShapeDtypeStruct((toks, peers * width), buf.dtype),
        in_specs=[VM],
        out_specs=ANY,
        scratch_shapes=[pltpu.VMEM((peers, toks, width), buf.dtype), pltpu.SemaphoreType.DMA((peers,))],
        compiler_params=params(16),
        name="unpack",
    )(buf)


def swap(x):
    return lax.all_to_all(x, "expert", split_axis=0, concat_axis=0, tiled=True)


def ring(x, blocks):
    ahead = [(i, (i - 1) % blocks) for i in range(blocks)]
    behind = [(i, (i + 1) % blocks) for i in range(blocks)]
    held = {0: x}
    for step in range(1, blocks // 2 + 1):
        held[step] = lax.ppermute(held[step - 1], "tensor", ahead)
        if 2 * step < blocks:
            held[blocks - step] = lax.ppermute(held[(blocks - step + 1) % blocks], "tensor", behind)
    return [held[k] for k in range(blocks)]


def per_device(tokens, routes, route_weight, shrink_weight, expand_weight):
    toks, _ = tokens.shape
    local, rank, _ = shrink_weight.shape
    peers = lax.axis_size("expert")
    blocks = lax.axis_size("tensor")
    rows = local * rank
    group = min(8, peers)
    packed = pack(tokens, shrink_weight.reshape(rows, -1), routes.T.reshape(1, -1), peers)
    packed, block = lax.optimization_barrier((packed, expand_weight.reshape(rows, -1)))
    arrived = swap(packed)
    placed = place(ring(block, blocks), peers, rank)
    arrived, placed = lax.optimization_barrier((arrived, placed))
    partial = shrink(arrived, toks, rows, rank, group)
    vectors = swap(combine(swap(partial), route_weight.T, placed))
    return unpack(swap(expand(vectors, arrived, rank, group)))


def solution(mesh):
    return jax.shard_map(
        per_device,
        mesh=mesh,
        in_specs=(
            P(("expert", "tensor"), None),
            P(("expert", "tensor"), None),
            P(("expert", "tensor"), None),
            P("expert", None, None),
            P("expert", None, "tensor"),
        ),
        out_specs=P(("expert", "tensor"), None),
        check_vma=False,
    )
```

```python
import functools

import jax
import jax.numpy as jnp
from jax import lax
from jax.experimental import pallas as pl
from jax.experimental.pallas import tpu as pltpu
from jax.sharding import PartitionSpec as P

BF16 = jnp.bfloat16
F32 = jnp.float32
ANY = pl.BlockSpec(memory_space=pl.ANY)
HBM = pl.BlockSpec(memory_space=pltpu.HBM)
VM = pl.BlockSpec(memory_space=pltpu.VMEM)
NT = (((1,), (1,)), ((), ()))
TILE = 16
LANES = 128


def params(mib):
    return pltpu.CompilerParams(vmem_limit_bytes=mib * 1024 * 1024)


def first_kernel(peers, blocks, toks, width, weight_ref, expand_ref, routes_ref, out_ref, sems):
    me = lax.axis_index("tensor")
    halves = width // LANES
    row = pl.multiple_of((me // halves) * TILE, TILE)
    copies = []
    for p in range(peers):
        col = pl.multiple_of(p * width + lax.rem(me, halves) * LANES, LANES)
        copy = pltpu.make_async_copy(
            weight_ref.at[pl.ds(row, TILE), pl.ds(col, LANES)], out_ref.at[p, pl.ds(0, TILE)], sems.at[p]
        )
        copy.start()
        copies.append(copy)
    names = routes_ref[...].astype(F32)
    names = jnp.concatenate([names, jnp.zeros((TILE - 2, toks), F32)], axis=0).astype(BF16)
    feats = expand_ref.shape[1] // peers
    for t in range(expand_ref.shape[1] // LANES):
        block = expand_ref[:, t * LANES : (t + 1) * LANES].astype(F32).T
        for j in range(LANES // feats):
            p = t * (LANES // feats) + j
            piece = block[j * feats : (j + 1) * feats]
            piece = jnp.concatenate([piece[:TILE], piece[TILE:]], axis=1)
            out_ref[p, pl.ds(TILE, TILE), :] = piece.astype(BF16)
            out_ref[p, pl.ds(2 * TILE, TILE), :] = names
    for copy in copies:
        copy.wait()


def pack_first(weight, expand_weight, routes, peers, blocks):
    width = weight.shape[1] // peers
    toks = routes.shape[1]
    return pl.pallas_call(
        functools.partial(first_kernel, peers, blocks, toks, width),
        out_shape=jax.ShapeDtypeStruct((peers, 3 * TILE, LANES), BF16),
        in_specs=[HBM, VM, VM],
        out_specs=VM,
        scratch_shapes=[pltpu.SemaphoreType.DMA((peers,))],
        compiler_params=params(56),
        name="pack_first",
    )(weight, expand_weight, routes)


def pack_kernel(peers, width, tokens_ref, out_ref, buf, sems):
    copies = []
    for p in range(peers):
        copy = pltpu.make_async_copy(tokens_ref.at[:, pl.ds(p * width, width)], buf.at[p], sems.at[0, p])
        copy.start()
        copies.append(copy)
    sends = []
    for p in range(peers):
        copies[p].wait()
        send = pltpu.make_async_copy(buf.at[p], out_ref.at[p], sems.at[1, p])
        send.start()
        sends.append(send)
    for send in sends:
        send.wait()


def pack(tokens, peers):
    toks, d = tokens.shape
    width = d // peers
    shape = (peers, toks, width)
    return pl.pallas_call(
        functools.partial(pack_kernel, peers, width),
        out_shape=jax.ShapeDtypeStruct(shape, tokens.dtype),
        in_specs=[HBM],
        out_specs=HBM,
        scratch_shapes=[pltpu.VMEM(shape, tokens.dtype), pltpu.SemaphoreType.DMA((2, peers))],
        compiler_params=params(56),
        name="pack",
    )(tokens)


def place_kernel(blocks, *refs):
    *held_refs, down_ref, up_ref, sems = refs
    halves = down_ref.shape[2] // LANES
    me = lax.axis_index("tensor")
    copies = []
    for k, ref in enumerate(held_refs):
        owner = lax.rem(me + k, blocks)
        row = pl.multiple_of((owner // halves) * TILE, TILE)
        col = pl.multiple_of(lax.rem(owner, halves) * LANES, LANES)
        copy = pltpu.make_async_copy(
            ref.at[:, pl.ds(0, TILE), :], down_ref.at[:, pl.ds(row, TILE), pl.ds(col, LANES)], sems.at[k]
        )
        copy.start()
        copies.append(copy)
    low = lax.broadcasted_iota(jnp.int32, (TILE, LANES), 1) < LANES // 2
    for k, ref in enumerate(held_refs):
        row = pl.multiple_of(lax.rem(me + k, blocks) * (2 * TILE), 2 * TILE)
        for t in range(ref.shape[0] // 2):
            a = ref[2 * t, pl.ds(TILE, TILE), :].astype(F32)
            b = ref[2 * t + 1, pl.ds(TILE, TILE), :].astype(F32)
            first = jnp.where(low, a, pltpu.roll(b, LANES // 2, 1))
            second = jnp.where(low, pltpu.roll(a, LANES // 2, 1), b)
            both = jnp.concatenate([first, second], axis=0).astype(BF16)
            up_ref[pl.ds(row, 2 * TILE), t * LANES : (t + 1) * LANES] = both
    for copy in copies:
        copy.wait()


def place(held, rows, width):
    peers = held[0].shape[0]
    blocks = len(held)
    return pl.pallas_call(
        functools.partial(place_kernel, blocks),
        out_shape=(
            jax.ShapeDtypeStruct((peers, rows, width), BF16),
            jax.ShapeDtypeStruct((blocks * 2 * TILE, peers * rows), BF16),
        ),
        in_specs=[VM] * blocks,
        out_specs=(VM, VM),
        scratch_shapes=[pltpu.SemaphoreType.DMA((blocks,))],
        compiler_params=params(16),
        name="place",
    )(*held)


def shrink_kernel(group, rank, x_ref, w_ref, r_ref, out_ref):
    peers, wrows, width = w_ref.shape
    toks = x_ref.shape[1]
    chunk = max(1, 256 // wrows)
    per = chunk * wrows // rank
    x = x_ref[...].reshape(group * toks, width)
    names = [r_ref[b].astype(F32) for b in range(group)]
    acc = [[jnp.zeros((rank, toks), F32) for _ in range(2)] for _ in range(group)]
    for c in range(peers // chunk):
        w = w_ref[c * chunk : (c + 1) * chunk].reshape(chunk * wrows, width)
        p = lax.dot_general(w, x, NT, preferred_element_type=F32)
        for j in range(per):
            e = c * per + j
            for b in range(group):
                piece = p[j * rank : (j + 1) * rank, b * toks : (b + 1) * toks]
                for k in range(2):
                    acc[b][k] = jnp.where(names[b][k : k + 1] == e, piece, acc[b][k])
    for b in range(group):
        for k in range(2):
            out_ref[b, pl.ds(k * rank, rank), :] = acc[b][k].astype(out_ref.dtype)


def shrink(tokens, weight, first, rank, group):
    peers, toks, width = tokens.shape
    return pl.pallas_call(
        functools.partial(shrink_kernel, group, rank),
        grid=(peers // group,),
        out_shape=jax.ShapeDtypeStruct((peers, 2 * rank, toks), BF16),
        in_specs=[
            pl.BlockSpec((group, toks, width), lambda i: (i, 0, 0)),
            pl.BlockSpec(weight.shape, lambda i: (0, 0, 0)),
            pl.BlockSpec((group, TILE, LANES), lambda i: (i, 2, 0)),
        ],
        out_specs=pl.BlockSpec((group, 2 * rank, toks), lambda i: (i, 0, 0)),
        compiler_params=params(14),
        name="shrink",
    )(tokens, weight, first)


def combine_kernel(peers, rank, part_ref, gate_ref, out_ref):
    gated = []
    for k in range(2):
        total = part_ref[0, pl.ds(k * rank, rank), :].astype(F32)
        for p in range(1, peers):
            total = total + part_ref[p, pl.ds(k * rank, rank), :].astype(F32)
        gated.append((total.astype(BF16).astype(F32) * gate_ref[pl.ds(k, 1), :]).astype(BF16))
    both = jnp.concatenate(gated, axis=1)
    for p in range(peers):
        out_ref[p] = both


def combine(part, gates):
    peers, rank2, toks = part.shape
    rank = rank2 // 2
    return pl.pallas_call(
        functools.partial(combine_kernel, peers, rank),
        out_shape=jax.ShapeDtypeStruct((peers, rank, 2 * toks), BF16),
        in_specs=[VM, VM],
        out_specs=VM,
        compiler_params=params(16),
        name="combine",
    )(part, gates)


def expand_kernel(group, experts, s_ref, r_ref, w_ref, out_ref):
    rank = s_ref.shape[1]
    toks = s_ref.shape[2] // 2
    spread = []
    for b in range(group):
        s = s_ref[b]
        names = r_ref[b]
        s0, s1 = s[:, :toks], s[:, toks:]
        r0, r1 = (jnp.broadcast_to(names[k : k + 1], (rank, toks)) for k in range(2))
        zero = jnp.zeros((rank, toks), BF16)
        rows = []
        for e in range(experts):
            name = jnp.asarray(e, BF16)
            rows.append(jnp.where(r0 == name, s0, jnp.where(r1 == name, s1, zero)))
        spread.append(jnp.concatenate(rows, axis=0))
    out = jnp.dot(w_ref[...], jnp.concatenate(spread, axis=1), preferred_element_type=F32)
    for b in range(group):
        out_ref[b] = out[:, b * toks : (b + 1) * toks].astype(BF16)


def expand(vectors, first, weight, rank, group):
    peers, _, toks2 = vectors.shape
    toks = toks2 // 2
    feats, cols = weight.shape
    return pl.pallas_call(
        functools.partial(expand_kernel, group, cols // rank),
        grid=(peers // group,),
        out_shape=jax.ShapeDtypeStruct((peers, feats, toks), BF16),
        in_specs=[
            pl.BlockSpec((group, rank, toks2), lambda i: (i, 0, 0)),
            pl.BlockSpec((group, TILE, LANES), lambda i: (i, 2, 0)),
            pl.BlockSpec(weight.shape, lambda i: (0, 0)),
        ],
        out_specs=pl.BlockSpec((group, feats, toks), lambda i: (i, 0, 0)),
        compiler_params=params(20),
        name="expand",
    )(vectors, first, weight)


def unpack_kernel(blocks, in_ref, out_ref, buf, sems):
    peers, feats, toks = in_ref.shape
    piece = feats // blocks
    per = LANES // piece
    cols = peers * piece
    copies = []
    for z in range(blocks):
        for q in range(peers // per):
            parts = [in_ref[per * q + k, z * piece : (z + 1) * piece, :] for k in range(per)]
            buf[z, q] = jnp.concatenate(parts, axis=0).T
            copy = pltpu.make_async_copy(
                buf.at[z, q], out_ref.at[:, pl.ds(z * cols + q * LANES, LANES)], sems.at[z, q]
            )
            copy.start()
            copies.append(copy)
    for copy in copies:
        copy.wait()


def unpack(buf, blocks):
    peers, feats, toks = buf.shape
    quads = peers * (feats // blocks) // LANES
    return pl.pallas_call(
        functools.partial(unpack_kernel, blocks),
        out_shape=jax.ShapeDtypeStruct((toks, peers * feats), buf.dtype),
        in_specs=[VM],
        out_specs=ANY,
        scratch_shapes=[
            pltpu.VMEM((blocks, quads, toks, LANES), buf.dtype),
            pltpu.SemaphoreType.DMA((blocks, quads)),
        ],
        compiler_params=params(16),
        name="unpack",
    )(buf)


def swap(x):
    return lax.all_to_all(x, "expert", split_axis=0, concat_axis=0, tiled=True)


def ring(x, blocks):
    ahead = [(i, (i - 1) % blocks) for i in range(blocks)]
    behind = [(i, (i + 1) % blocks) for i in range(blocks)]
    held = {0: x}
    for step in range(1, blocks // 2 + 1):
        held[step] = lax.ppermute(held[step - 1], "tensor", ahead)
        if 2 * step < blocks:
            held[blocks - step] = lax.ppermute(held[(blocks - step + 1) % blocks], "tensor", behind)
    return [held[k] for k in range(blocks)]


def per_device(tokens, routes, route_weight, shrink_weight, expand_weight):
    local, rank, features = shrink_weight.shape
    peers = lax.axis_size("expert")
    blocks = lax.axis_size("tensor")
    rows = local * rank
    group = min(8, peers)
    first = swap(
        pack_first(shrink_weight.reshape(rows, -1), expand_weight.reshape(rows, -1), routes.T, peers, blocks)
    )
    arrived = swap(pack(tokens, peers))
    held = ring(first[:, : 2 * TILE], blocks)
    arrived, (down, up) = lax.optimization_barrier((arrived, place(held, rows, features // peers)))
    partial = shrink(arrived, down, first, rank, group)
    vectors = swap(combine(swap(partial), route_weight.T))
    return unpack(swap(expand(vectors, first, up, rank, group)), blocks)


def solution(mesh):
    return jax.shard_map(
        per_device,
        mesh=mesh,
        in_specs=(
            P(("expert", "tensor"), None),
            P(("expert", "tensor"), None),
            P(("expert", "tensor"), None),
            P("expert", None, None),
            P("expert", None, "tensor"),
        ),
        out_specs=P(("expert", "tensor"), None),
        check_vma=False,
    )
```

```python
import functools

import jax
import jax.numpy as jnp
from jax import lax
from jax.experimental import pallas as pl
from jax.experimental.pallas import tpu as pltpu
from jax.sharding import PartitionSpec as P

BF16 = jnp.bfloat16
F32 = jnp.float32
ANY = pl.BlockSpec(memory_space=pl.ANY)
HBM = pl.BlockSpec(memory_space=pltpu.HBM)
VM = pl.BlockSpec(memory_space=pltpu.VMEM)
NT = (((1,), (1,)), ((), ()))
TILE = 16
LANES = 128


def params(mib):
    return pltpu.CompilerParams(vmem_limit_bytes=mib * 1024 * 1024)


def first_kernel(peers, blocks, toks, width, weight_ref, expand_hbm, routes_hbm, out_ref, expand_ref, routes_ref, sems):
    me = lax.axis_index("tensor")
    halves = width // LANES
    row = pl.multiple_of((me // halves) * TILE, TILE)
    reads = [
        pltpu.make_async_copy(expand_hbm, expand_ref, sems.at[peers]),
        pltpu.make_async_copy(routes_hbm, routes_ref, sems.at[peers + 1]),
    ]
    for read in reads:
        read.start()
    copies = []
    for p in range(peers):
        col = pl.multiple_of(p * width + lax.rem(me, halves) * LANES, LANES)
        copy = pltpu.make_async_copy(
            weight_ref.at[pl.ds(row, TILE), pl.ds(col, LANES)], out_ref.at[p, pl.ds(0, TILE)], sems.at[p]
        )
        copy.start()
        copies.append(copy)
    for read in reads:
        read.wait()
    names = routes_ref[...].astype(F32)
    names = jnp.concatenate([names, jnp.zeros((TILE - 2, toks), F32)], axis=0).astype(BF16)
    feats = expand_ref.shape[1] // peers
    for t in range(expand_ref.shape[1] // LANES):
        block = expand_ref[:, t * LANES : (t + 1) * LANES].astype(F32).T
        for j in range(LANES // feats):
            p = t * (LANES // feats) + j
            piece = block[j * feats : (j + 1) * feats]
            piece = jnp.concatenate([piece[:TILE], piece[TILE:]], axis=1)
            out_ref[p, pl.ds(TILE, TILE), :] = piece.astype(BF16)
            out_ref[p, pl.ds(2 * TILE, TILE), :] = names
    for copy in copies:
        copy.wait()


def pack_first(weight, expand_weight, routes, peers, blocks):
    width = weight.shape[1] // peers
    toks = routes.shape[1]
    return pl.pallas_call(
        functools.partial(first_kernel, peers, blocks, toks, width),
        out_shape=jax.ShapeDtypeStruct((peers, 3 * TILE, LANES), BF16),
        in_specs=[HBM, HBM, HBM],
        out_specs=VM,
        scratch_shapes=[
            pltpu.VMEM(expand_weight.shape, BF16),
            pltpu.VMEM(routes.shape, routes.dtype),
            pltpu.SemaphoreType.DMA((peers + 2,)),
        ],
        compiler_params=params(56),
        name="pack_first",
    )(weight, expand_weight, routes)


def pack_kernel(peers, width, tokens_ref, out_ref, buf, sems):
    copies = []
    for p in range(peers):
        copy = pltpu.make_async_copy(tokens_ref.at[:, pl.ds(p * width, width)], buf.at[p], sems.at[0, p])
        copy.start()
        copies.append(copy)
    sends = []
    for p in range(peers):
        copies[p].wait()
        send = pltpu.make_async_copy(buf.at[p], out_ref.at[p], sems.at[1, p])
        send.start()
        sends.append(send)
    for send in sends:
        send.wait()


def pack(tokens, peers):
    toks, d = tokens.shape
    width = d // peers
    shape = (peers, toks, width)
    return pl.pallas_call(
        functools.partial(pack_kernel, peers, width),
        out_shape=jax.ShapeDtypeStruct(shape, tokens.dtype),
        in_specs=[HBM],
        out_specs=HBM,
        scratch_shapes=[pltpu.VMEM(shape, tokens.dtype), pltpu.SemaphoreType.DMA((2, peers))],
        compiler_params=params(56),
        name="pack",
    )(tokens)


def place_kernel(blocks, *refs):
    *held_refs, down_ref, up_ref, sems = refs
    held_refs, more_refs = held_refs[:blocks], held_refs[blocks:]
    halves = down_ref.shape[2] // LANES
    me = lax.axis_index("tensor")
    copies = []
    for k, ref in enumerate(held_refs):
        owner = lax.rem(me + k, blocks)
        row = pl.multiple_of((owner // halves) * TILE, TILE)
        col = pl.multiple_of(lax.rem(owner, halves) * LANES, LANES)
        copy = pltpu.make_async_copy(
            ref, down_ref.at[:, pl.ds(row, TILE), pl.ds(col, LANES)], sems.at[k]
        )
        copy.start()
        copies.append(copy)
    low = lax.broadcasted_iota(jnp.int32, (TILE, LANES), 1) < LANES // 2
    for k, ref in enumerate(more_refs):
        row = pl.multiple_of(lax.rem(me + k, blocks) * (2 * TILE), 2 * TILE)
        for t in range(ref.shape[0] // 2):
            a = ref[2 * t].astype(F32)
            b = ref[2 * t + 1].astype(F32)
            first = jnp.where(low, a, pltpu.roll(b, LANES // 2, 1))
            second = jnp.where(low, pltpu.roll(a, LANES // 2, 1), b)
            both = jnp.concatenate([first, second], axis=0).astype(BF16)
            up_ref[pl.ds(row, 2 * TILE), t * LANES : (t + 1) * LANES] = both
    for copy in copies:
        copy.wait()


def place(held, more, rows, width):
    peers = held[0].shape[0]
    blocks = len(held)
    return pl.pallas_call(
        functools.partial(place_kernel, blocks),
        out_shape=(
            jax.ShapeDtypeStruct((peers, rows, width), BF16),
            jax.ShapeDtypeStruct((blocks * 2 * TILE, peers * rows), BF16),
        ),
        in_specs=[VM] * (2 * blocks),
        out_specs=(VM, VM),
        scratch_shapes=[pltpu.SemaphoreType.DMA((blocks,))],
        compiler_params=params(16),
        name="place",
    )(*held, *more)


def shrink_kernel(group, rank, x_ref, w_ref, r_ref, out_ref):
    peers, wrows, width = w_ref.shape
    toks = x_ref.shape[1]
    chunk = max(1, 256 // wrows)
    per = chunk * wrows // rank
    x = x_ref[...].reshape(group * toks, width)
    names = [r_ref[b].astype(F32) for b in range(group)]
    acc = [[jnp.zeros((rank, toks), F32) for _ in range(2)] for _ in range(group)]
    for c in range(peers // chunk):
        w = w_ref[c * chunk : (c + 1) * chunk].reshape(chunk * wrows, width)
        p = lax.dot_general(w, x, NT, preferred_element_type=F32)
        for j in range(per):
            e = c * per + j
            for b in range(group):
                piece = p[j * rank : (j + 1) * rank, b * toks : (b + 1) * toks]
                for k in range(2):
                    acc[b][k] = jnp.where(names[b][k : k + 1] == e, piece, acc[b][k])
    for b in range(group):
        for k in range(2):
            out_ref[b, pl.ds(k * rank, rank), :] = acc[b][k].astype(out_ref.dtype)


def shrink(tokens, weight, first, rank, group):
    peers, toks, width = tokens.shape
    return pl.pallas_call(
        functools.partial(shrink_kernel, group, rank),
        grid=(peers // group,),
        out_shape=jax.ShapeDtypeStruct((peers, 2 * rank, toks), BF16),
        in_specs=[
            pl.BlockSpec((group, toks, width), lambda i: (i, 0, 0)),
            pl.BlockSpec(weight.shape, lambda i: (0, 0, 0)),
            pl.BlockSpec((group, TILE, LANES), lambda i: (i, 2, 0)),
        ],
        out_specs=pl.BlockSpec((group, 2 * rank, toks), lambda i: (i, 0, 0)),
        compiler_params=params(14),
        name="shrink",
    )(tokens, weight, first)


def combine_kernel(peers, rank, part_ref, gate_ref, out_ref):
    gated = []
    for k in range(2):
        total = part_ref[0, pl.ds(k * rank, rank), :].astype(F32)
        for p in range(1, peers):
            total = total + part_ref[p, pl.ds(k * rank, rank), :].astype(F32)
        gated.append((total.astype(BF16).astype(F32) * gate_ref[pl.ds(k, 1), :]).astype(BF16))
    both = jnp.concatenate(gated, axis=1)
    for p in range(peers):
        out_ref[p] = both


def combine(part, gates):
    peers, rank2, toks = part.shape
    rank = rank2 // 2
    return pl.pallas_call(
        functools.partial(combine_kernel, peers, rank),
        out_shape=jax.ShapeDtypeStruct((peers, rank, 2 * toks), BF16),
        in_specs=[VM, VM],
        out_specs=VM,
        compiler_params=params(16),
        name="combine",
    )(part, gates)


def expand_kernel(group, experts, s_ref, r_ref, w_ref, out_ref):
    rank = s_ref.shape[1]
    toks = s_ref.shape[2] // 2
    spread = []
    for b in range(group):
        s = s_ref[b]
        names = r_ref[b]
        s0, s1 = s[:, :toks], s[:, toks:]
        r0, r1 = (jnp.broadcast_to(names[k : k + 1], (rank, toks)) for k in range(2))
        zero = jnp.zeros((rank, toks), BF16)
        rows = []
        for e in range(experts):
            name = jnp.asarray(e, BF16)
            rows.append(jnp.where(r0 == name, s0, jnp.where(r1 == name, s1, zero)))
        spread.append(jnp.concatenate(rows, axis=0))
    out = jnp.dot(w_ref[...], jnp.concatenate(spread, axis=1), preferred_element_type=F32)
    for b in range(group):
        out_ref[b] = out[:, b * toks : (b + 1) * toks].astype(BF16)


def expand(vectors, first, weight, rank, group):
    peers, _, toks2 = vectors.shape
    toks = toks2 // 2
    feats, cols = weight.shape
    return pl.pallas_call(
        functools.partial(expand_kernel, group, cols // rank),
        grid=(peers // group,),
        out_shape=jax.ShapeDtypeStruct((peers, feats, toks), BF16),
        in_specs=[
            pl.BlockSpec((group, rank, toks2), lambda i: (i, 0, 0)),
            pl.BlockSpec((group, TILE, LANES), lambda i: (i, 2, 0)),
            pl.BlockSpec(weight.shape, lambda i: (0, 0)),
        ],
        out_specs=pl.BlockSpec((group, feats, toks), lambda i: (i, 0, 0)),
        compiler_params=params(20),
        name="expand",
    )(vectors, first, weight)


def unpack_kernel(blocks, in_ref, out_ref, buf, sems):
    peers, feats, toks = in_ref.shape
    piece = feats // blocks
    per = LANES // piece
    cols = peers * piece
    copies = []
    for z in range(blocks):
        for q in range(peers // per):
            parts = [in_ref[per * q + k, z * piece : (z + 1) * piece, :] for k in range(per)]
            buf[z, q] = jnp.concatenate(parts, axis=0).T
            copy = pltpu.make_async_copy(
                buf.at[z, q], out_ref.at[:, pl.ds(z * cols + q * LANES, LANES)], sems.at[z, q]
            )
            copy.start()
            copies.append(copy)
    for copy in copies:
        copy.wait()


def unpack(buf, blocks):
    peers, feats, toks = buf.shape
    quads = peers * (feats // blocks) // LANES
    return pl.pallas_call(
        functools.partial(unpack_kernel, blocks),
        out_shape=jax.ShapeDtypeStruct((toks, peers * feats), buf.dtype),
        in_specs=[VM],
        out_specs=ANY,
        scratch_shapes=[
            pltpu.VMEM((blocks, quads, toks, LANES), buf.dtype),
            pltpu.SemaphoreType.DMA((blocks, quads)),
        ],
        compiler_params=params(16),
        name="unpack",
    )(buf)


def swap(x):
    return lax.all_to_all(x, "expert", split_axis=0, concat_axis=0, tiled=True)


def ring(x, blocks):
    ahead = [(i, (i - 1) % blocks) for i in range(blocks)]
    behind = [(i, (i + 1) % blocks) for i in range(blocks)]
    held = {0: x}
    for step in range(1, blocks // 2 + 1):
        held[step] = lax.ppermute(held[step - 1], "tensor", ahead)
        if 2 * step < blocks:
            held[blocks - step] = lax.ppermute(held[(blocks - step + 1) % blocks], "tensor", behind)
    return [held[k] for k in range(blocks)]


def per_device(tokens, routes, route_weight, shrink_weight, expand_weight):
    local, rank, features = shrink_weight.shape
    peers = lax.axis_size("expert")
    blocks = lax.axis_size("tensor")
    rows = local * rank
    group = min(8, peers)
    first = swap(
        pack_first(shrink_weight.reshape(rows, -1), expand_weight.reshape(rows, -1), routes.T, peers, blocks)
    )
    arrived = swap(pack(tokens, peers))
    downs, ups = ring(first[:, :TILE], blocks), ring(first[:, TILE : 2 * TILE], blocks)
    arrived, last = lax.optimization_barrier((arrived, downs[-1]))
    down, up = place(downs[:-1] + [last], ups, rows, features // peers)
    partial = shrink(arrived, down, first, rank, group)
    vectors = swap(combine(swap(partial), route_weight.T))
    return unpack(swap(expand(vectors, first, up, rank, group)), blocks)


def solution(mesh):
    return jax.shard_map(
        per_device,
        mesh=mesh,
        in_specs=(
            P(("expert", "tensor"), None),
            P(("expert", "tensor"), None),
            P(("expert", "tensor"), None),
            P("expert", None, None),
            P("expert", None, "tensor"),
        ),
        out_specs=P(("expert", "tensor"), None),
        check_vma=False,
    )
```

```python
import functools

import jax
import jax.numpy as jnp
from jax import lax
from jax.experimental import pallas as pl
from jax.experimental.pallas import tpu as pltpu
from jax.sharding import PartitionSpec as P

BF16 = jnp.bfloat16
F32 = jnp.float32
ANY = pl.BlockSpec(memory_space=pl.ANY)
HBM = pl.BlockSpec(memory_space=pltpu.HBM)
VM = pl.BlockSpec(memory_space=pltpu.VMEM)
NT = (((1,), (1,)), ((), ()))
TILE = 16
LANES = 128


def params(mib):
    return pltpu.CompilerParams(vmem_limit_bytes=mib * 1024 * 1024)


def first_kernel(peers, blocks, toks, width, weight_ref, expand_hbm, routes_hbm, out_ref, expand_ref, routes_ref, sems):
    me = lax.axis_index("tensor")
    halves = width // LANES
    row = pl.multiple_of((me // halves) * TILE, TILE)
    reads = [
        pltpu.make_async_copy(expand_hbm, expand_ref, sems.at[peers]),
        pltpu.make_async_copy(routes_hbm, routes_ref, sems.at[peers + 1]),
    ]
    for read in reads:
        read.start()
    copies = []
    for p in range(peers):
        col = pl.multiple_of(p * width + lax.rem(me, halves) * LANES, LANES)
        copy = pltpu.make_async_copy(
            weight_ref.at[pl.ds(row, TILE), pl.ds(col, LANES)], out_ref.at[p, pl.ds(0, TILE)], sems.at[p]
        )
        copy.start()
        copies.append(copy)
    for read in reads:
        read.wait()
    names = routes_ref[...].astype(F32)
    names = jnp.concatenate([names, jnp.zeros((TILE - 2, toks), F32)], axis=0).astype(BF16)
    feats = expand_ref.shape[1] // peers
    for t in range(expand_ref.shape[1] // LANES):
        block = expand_ref[:, t * LANES : (t + 1) * LANES].astype(F32).T
        for j in range(LANES // feats):
            p = t * (LANES // feats) + j
            piece = block[j * feats : (j + 1) * feats]
            piece = jnp.concatenate([piece[:TILE], piece[TILE:]], axis=1)
            out_ref[p, pl.ds(TILE, TILE), :] = piece.astype(BF16)
            out_ref[p, pl.ds(2 * TILE, TILE), :] = names
    for copy in copies:
        copy.wait()


def pack_first(weight, expand_weight, routes, peers, blocks):
    width = weight.shape[1] // peers
    toks = routes.shape[1]
    return pl.pallas_call(
        functools.partial(first_kernel, peers, blocks, toks, width),
        out_shape=jax.ShapeDtypeStruct((peers, 3 * TILE, LANES), BF16),
        in_specs=[HBM, HBM, HBM],
        out_specs=VM,
        scratch_shapes=[
            pltpu.VMEM(expand_weight.shape, BF16),
            pltpu.VMEM(routes.shape, routes.dtype),
            pltpu.SemaphoreType.DMA((peers + 2,)),
        ],
        compiler_params=params(56),
        name="pack_first",
    )(weight, expand_weight, routes)


def pack_kernel(chips, width, tokens_ref, out_ref, buf, sems):
    core = lax.rem(lax.axis_index("expert"), 2)
    copies = []
    for p in range(chips):
        pair = []
        for h in range(2):
            side = core if h == 0 else 1 - core
            col = pl.multiple_of((2 * p + side) * width, LANES)
            copy = pltpu.make_async_copy(
                tokens_ref.at[:, pl.ds(col, width)], buf.at[p, :, pl.ds(h * width, width)], sems.at[h, p]
            )
            copy.start()
            pair.append(copy)
        copies.append(pair)
    sends = []
    for p in range(chips):
        for copy in copies[p]:
            copy.wait()
        send = pltpu.make_async_copy(buf.at[p], out_ref.at[p], sems.at[2, p])
        send.start()
        sends.append(send)
    for send in sends:
        send.wait()


def pack(tokens, chips):
    toks, d = tokens.shape
    width = d // chips // 2
    shape = (chips, toks, 2 * width)
    return pl.pallas_call(
        functools.partial(pack_kernel, chips, width),
        out_shape=jax.ShapeDtypeStruct(shape, tokens.dtype),
        in_specs=[HBM],
        out_specs=HBM,
        scratch_shapes=[pltpu.VMEM(shape, tokens.dtype), pltpu.SemaphoreType.DMA((3, chips))],
        compiler_params=params(56),
        name="pack",
    )(tokens)


def place_kernel(blocks, *refs):
    *held_refs, down_ref, up_ref, sems = refs
    held_refs, more_refs = held_refs[:blocks], held_refs[blocks:]
    halves = down_ref.shape[2] // LANES
    me = lax.axis_index("tensor")
    copies = []
    for k, ref in enumerate(held_refs):
        owner = lax.rem(me + k, blocks)
        row = pl.multiple_of((owner // halves) * TILE, TILE)
        col = pl.multiple_of(lax.rem(owner, halves) * LANES, LANES)
        copy = pltpu.make_async_copy(
            ref, down_ref.at[:, pl.ds(row, TILE), pl.ds(col, LANES)], sems.at[k]
        )
        copy.start()
        copies.append(copy)
    low = lax.broadcasted_iota(jnp.int32, (TILE, LANES), 1) < LANES // 2
    for k, ref in enumerate(more_refs):
        row = pl.multiple_of(lax.rem(me + k, blocks) * (2 * TILE), 2 * TILE)
        for t in range(ref.shape[0] // 2):
            a = ref[2 * t].astype(F32)
            b = ref[2 * t + 1].astype(F32)
            first = jnp.where(low, a, pltpu.roll(b, LANES // 2, 1))
            second = jnp.where(low, pltpu.roll(a, LANES // 2, 1), b)
            both = jnp.concatenate([first, second], axis=0).astype(BF16)
            up_ref[pl.ds(row, 2 * TILE), t * LANES : (t + 1) * LANES] = both
    for copy in copies:
        copy.wait()


def place(held, more, rows, width):
    peers = held[0].shape[0]
    blocks = len(held)
    return pl.pallas_call(
        functools.partial(place_kernel, blocks),
        out_shape=(
            jax.ShapeDtypeStruct((peers, rows, width), BF16),
            jax.ShapeDtypeStruct((blocks * 2 * TILE, peers * rows), BF16),
        ),
        in_specs=[VM] * (2 * blocks),
        out_specs=(VM, VM),
        scratch_shapes=[pltpu.SemaphoreType.DMA((blocks,))],
        compiler_params=params(16),
        name="place",
    )(*held, *more)


def shrink_kernel(group, rank, x_ref, w_ref, r_ref, *refs):
    *base_refs, out_ref = refs
    peers, wrows, width = w_ref.shape
    toks = x_ref.shape[1]
    chunk = max(1, 256 // wrows)
    per = chunk * wrows // rank
    x = x_ref[...].reshape(group * toks, width)
    names = [r_ref[b].astype(F32) for b in range(group)]
    acc = [[jnp.zeros((rank, toks), F32) for _ in range(2)] for _ in range(group)]
    for c in range(peers // chunk):
        w = w_ref[c * chunk : (c + 1) * chunk].reshape(chunk * wrows, width)
        p = lax.dot_general(w, x, NT, preferred_element_type=F32)
        for j in range(per):
            e = c * per + j
            for b in range(group):
                piece = p[j * rank : (j + 1) * rank, b * toks : (b + 1) * toks]
                for k in range(2):
                    acc[b][k] = jnp.where(names[b][k : k + 1] == e, piece, acc[b][k])
    for b in range(group):
        for k in range(2):
            part = acc[b][k]
            for base in base_refs:
                part = part + base[b, pl.ds(k * rank, rank), :]
            out_ref[b, pl.ds(k * rank, rank), :] = part.astype(out_ref.dtype)


def shrink(tokens, weight, names, half, base, rank, group, dtype):
    chips, toks, width2 = tokens.shape
    width = width2 // 2
    sums = pl.BlockSpec((group, 2 * rank, toks), lambda i: (i, 0, 0))
    return pl.pallas_call(
        functools.partial(shrink_kernel, group, rank),
        grid=(chips // group,),
        out_shape=jax.ShapeDtypeStruct((chips, 2 * rank, toks), dtype),
        in_specs=[
            pl.BlockSpec((group, toks, width), lambda i: (i, 0, half)),
            pl.BlockSpec(weight.shape, lambda i: (0, 0, 0)),
            pl.BlockSpec((group, TILE, LANES), lambda i: (i, 0, 0)),
        ]
        + [sums] * len(base),
        out_specs=sums,
        compiler_params=params(14),
        cost_estimate=pl.CostEstimate(
            flops=2 * chips * toks * width * weight.shape[0] * weight.shape[1],
            bytes_accessed=2 * (chips * toks * width + weight.size),
            transcendentals=0,
        ),
        name="shrink",
    )(tokens, weight, names, *base)


def combine_kernel(peers, rank, part_ref, gate_ref, out_ref):
    gated = []
    for k in range(2):
        total = part_ref[0, pl.ds(k * rank, rank), :].astype(F32)
        for p in range(1, peers):
            total = total + part_ref[p, pl.ds(k * rank, rank), :].astype(F32)
        gated.append((total.astype(BF16).astype(F32) * gate_ref[pl.ds(k, 1), :]).astype(BF16))
    both = jnp.concatenate(gated, axis=1)
    for p in range(peers):
        out_ref[p] = both


def combine(part, gates):
    peers, rank2, toks = part.shape
    rank = rank2 // 2
    return pl.pallas_call(
        functools.partial(combine_kernel, peers, rank),
        out_shape=jax.ShapeDtypeStruct((peers, rank, 2 * toks), BF16),
        in_specs=[VM, VM],
        out_specs=VM,
        compiler_params=params(16),
        name="combine",
    )(part, gates)


def expand_kernel(group, experts, s_ref, r_ref, own_ref, other_ref, out_ref):
    rank = s_ref.shape[1]
    toks = s_ref.shape[2] // 2
    feats = own_ref.shape[0]
    spread = []
    for b in range(group):
        s = s_ref[b]
        names = r_ref[b]
        s0, s1 = s[:, :toks], s[:, toks:]
        r0, r1 = (jnp.broadcast_to(names[k : k + 1], (rank, toks)) for k in range(2))
        zero = jnp.zeros((rank, toks), BF16)
        rows = []
        for e in range(experts):
            name = jnp.asarray(e, BF16)
            rows.append(jnp.where(r0 == name, s0, jnp.where(r1 == name, s1, zero)))
        spread.append(jnp.concatenate(rows, axis=0))
    spread = jnp.concatenate(spread, axis=1)
    for h, w_ref in enumerate((own_ref, other_ref)):
        out = jnp.dot(w_ref[...], spread, preferred_element_type=F32)
        for b in range(group):
            out_ref[b, pl.ds(h * feats, feats), :] = out[:, b * toks : (b + 1) * toks].astype(BF16)


def expand(vectors, names, own, other, rank, group):
    chips, _, toks2 = vectors.shape
    toks = toks2 // 2
    feats, cols = own.shape
    return pl.pallas_call(
        functools.partial(expand_kernel, group, cols // rank),
        grid=(chips // group,),
        out_shape=jax.ShapeDtypeStruct((chips, 2 * feats, toks), BF16),
        in_specs=[
            pl.BlockSpec((group, rank, toks2), lambda i: (i, 0, 0)),
            pl.BlockSpec((group, TILE, LANES), lambda i: (i, 0, 0)),
            pl.BlockSpec(own.shape, lambda i: (0, 0)),
            pl.BlockSpec(other.shape, lambda i: (0, 0)),
        ],
        out_specs=pl.BlockSpec((group, 2 * feats, toks), lambda i: (i, 0, 0)),
        compiler_params=params(24),
        name="expand",
    )(vectors, names, own, other)


def unpack_kernel(blocks, in_ref, out_ref, buf, sems):
    chips, feats2, toks = in_ref.shape
    feats = feats2 // 2
    piece = feats // blocks
    per = LANES // piece // 2
    cols = 2 * chips * piece
    core = lax.rem(lax.axis_index("expert"), 2)
    copies = []
    for z in range(blocks):
        for q in range(chips // per):
            parts = []
            for k in range(per):
                for side in range(2):
                    half = core if side == 0 else 1 - core
                    row = pl.multiple_of(half * feats + z * piece, piece)
                    parts.append(in_ref[per * q + k, pl.ds(row, piece), :])
            buf[z, q] = jnp.concatenate(parts, axis=0).T
            copy = pltpu.make_async_copy(
                buf.at[z, q], out_ref.at[:, pl.ds(z * cols + q * LANES, LANES)], sems.at[z, q]
            )
            copy.start()
            copies.append(copy)
    for copy in copies:
        copy.wait()


def unpack(buf, blocks):
    chips, feats2, toks = buf.shape
    quads = chips * (feats2 // blocks) // LANES
    return pl.pallas_call(
        functools.partial(unpack_kernel, blocks),
        out_shape=jax.ShapeDtypeStruct((toks, chips * feats2), buf.dtype),
        in_specs=[VM],
        out_specs=ANY,
        scratch_shapes=[
            pltpu.VMEM((blocks, quads, toks, LANES), buf.dtype),
            pltpu.SemaphoreType.DMA((blocks, quads)),
        ],
        compiler_params=params(16),
        name="unpack",
    )(buf)


def swap(x):
    return lax.all_to_all(x, "expert", split_axis=0, concat_axis=0, tiled=True)


def swap_chips(x):
    chips = x.shape[0]
    groups = [[2 * q + core for q in range(chips)] for core in range(2)]
    return lax.all_to_all(x, "expert", split_axis=0, concat_axis=0, axis_index_groups=groups, tiled=True)


def sibling(x, peers):
    return lax.ppermute(x, "expert", [(i, i ^ 1) for i in range(peers)])


def ring(x, blocks):
    ahead = [(i, (i - 1) % blocks) for i in range(blocks)]
    behind = [(i, (i + 1) % blocks) for i in range(blocks)]
    held = {0: x}
    for step in range(1, blocks // 2 + 1):
        held[step] = lax.ppermute(held[step - 1], "tensor", ahead)
        if 2 * step < blocks:
            held[blocks - step] = lax.ppermute(held[(blocks - step + 1) % blocks], "tensor", behind)
    return [held[k] for k in range(blocks)]


def per_device(tokens, routes, route_weight, shrink_weight, expand_weight):
    local, rank, features = shrink_weight.shape
    peers = lax.axis_size("expert")
    blocks = lax.axis_size("tensor")
    rows = local * rank
    chips = peers // 2
    group = min(8, chips)
    core = lax.rem(lax.axis_index("expert"), 2)
    first = swap(
        pack_first(shrink_weight.reshape(rows, -1), expand_weight.reshape(rows, -1), routes.T, peers, blocks)
    )
    arrived = swap_chips(pack(tokens, chips))
    names = first.reshape(chips, 2, 3 * TILE, LANES)[:, :, 2 * TILE :]
    names = lax.dynamic_index_in_dim(names, core, 1, keepdims=False)
    downs, ups = ring(first[:, :TILE], blocks), ring(first[:, TILE : 2 * TILE], blocks)
    down, up = place(downs, ups, rows, features // peers)
    other_down, other_up = sibling(down, peers), sibling(up, peers)
    own = shrink(arrived, down, names, 0, [], rank, group, F32)
    partial = shrink(arrived, other_down, names, 1, [own], rank, group, BF16)
    vectors = swap_chips(combine(swap_chips(partial), route_weight.T))
    return unpack(swap_chips(expand(vectors, names, up, other_up, rank, group)), blocks)


def solution(mesh):
    return jax.shard_map(
        per_device,
        mesh=mesh,
        in_specs=(
            P(("expert", "tensor"), None),
            P(("expert", "tensor"), None),
            P(("expert", "tensor"), None),
            P("expert", None, None),
            P("expert", None, "tensor"),
        ),
        out_specs=P(("expert", "tensor"), None),
        check_vma=False,
    )
```

```python
import functools

import jax
import jax.numpy as jnp
from jax import lax
from jax.experimental import pallas as pl
from jax.experimental.pallas import tpu as pltpu
from jax.sharding import PartitionSpec as P

BF16 = jnp.bfloat16
F32 = jnp.float32
ANY = pl.BlockSpec(memory_space=pl.ANY)
HBM = pl.BlockSpec(memory_space=pltpu.HBM)
VM = pl.BlockSpec(memory_space=pltpu.VMEM)
NT = (((1,), (1,)), ((), ()))
TILE = 16
LANES = 128


def params(mib):
    return pltpu.CompilerParams(vmem_limit_bytes=mib * 1024 * 1024)


def first_kernel(peers, blocks, toks, width, weight_ref, expand_hbm, routes_hbm, out_ref, expand_ref, routes_ref, sems):
    me = lax.axis_index("tensor")
    halves = width // LANES
    row = pl.multiple_of((me // halves) * TILE, TILE)
    reads = [
        pltpu.make_async_copy(expand_hbm, expand_ref, sems.at[peers]),
        pltpu.make_async_copy(routes_hbm, routes_ref, sems.at[peers + 1]),
    ]
    for read in reads:
        read.start()
    copies = []
    for p in range(peers):
        col = pl.multiple_of(p * width + lax.rem(me, halves) * LANES, LANES)
        copy = pltpu.make_async_copy(
            weight_ref.at[pl.ds(row, TILE), pl.ds(col, LANES)], out_ref.at[p, pl.ds(0, TILE)], sems.at[p]
        )
        copy.start()
        copies.append(copy)
    for read in reads:
        read.wait()
    names = routes_ref[...].astype(F32)
    names = jnp.concatenate([names, jnp.zeros((TILE - 2, toks), F32)], axis=0).astype(BF16)
    feats = expand_ref.shape[1] // peers
    for t in range(expand_ref.shape[1] // LANES):
        block = expand_ref[:, t * LANES : (t + 1) * LANES].astype(F32).T
        for j in range(LANES // feats):
            p = t * (LANES // feats) + j
            piece = block[j * feats : (j + 1) * feats]
            piece = jnp.concatenate([piece[:TILE], piece[TILE:]], axis=1)
            out_ref[p, pl.ds(TILE, TILE), :] = piece.astype(BF16)
            out_ref[p, pl.ds(2 * TILE, TILE), :] = names
    for copy in copies:
        copy.wait()


def pack_first(weight, expand_weight, routes, peers, blocks):
    width = weight.shape[1] // peers
    toks = routes.shape[1]
    return pl.pallas_call(
        functools.partial(first_kernel, peers, blocks, toks, width),
        out_shape=jax.ShapeDtypeStruct((peers, 3 * TILE, LANES), BF16),
        in_specs=[HBM, HBM, HBM],
        out_specs=VM,
        scratch_shapes=[
            pltpu.VMEM(expand_weight.shape, BF16),
            pltpu.VMEM(routes.shape, routes.dtype),
            pltpu.SemaphoreType.DMA((peers + 2,)),
        ],
        compiler_params=params(56),
        name="pack_first",
    )(weight, expand_weight, routes)


def pack_kernel(chips, width, tokens_ref, out_ref, buf, sems):
    core = lax.rem(lax.axis_index("expert"), 2)
    copies = []
    for p in range(chips):
        pair = []
        for h in range(2):
            side = core if h == 0 else 1 - core
            col = pl.multiple_of((2 * p + side) * width, LANES)
            copy = pltpu.make_async_copy(
                tokens_ref.at[:, pl.ds(col, width)], buf.at[p, :, pl.ds(h * width, width)], sems.at[h, p]
            )
            copy.start()
            pair.append(copy)
        copies.append(pair)
    sends = []
    for p in range(chips):
        for copy in copies[p]:
            copy.wait()
        send = pltpu.make_async_copy(buf.at[p], out_ref.at[p], sems.at[2, p])
        send.start()
        sends.append(send)
    for send in sends:
        send.wait()


def pack(tokens, chips):
    toks, d = tokens.shape
    width = d // chips // 2
    shape = (chips, toks, 2 * width)
    return pl.pallas_call(
        functools.partial(pack_kernel, chips, width),
        out_shape=jax.ShapeDtypeStruct(shape, tokens.dtype),
        in_specs=[HBM],
        out_specs=HBM,
        scratch_shapes=[pltpu.VMEM(shape, tokens.dtype), pltpu.SemaphoreType.DMA((3, chips))],
        compiler_params=params(56),
        name="pack",
    )(tokens)


def place_kernel(blocks, *refs):
    *held_refs, down_ref, up_ref, sems = refs
    held_refs, more_refs = held_refs[:blocks], held_refs[blocks:]
    halves = down_ref.shape[2] // LANES
    me = lax.axis_index("tensor")
    copies = []
    for k, ref in enumerate(held_refs):
        owner = lax.rem(me + k, blocks)
        row = pl.multiple_of((owner // halves) * TILE, TILE)
        col = pl.multiple_of(lax.rem(owner, halves) * LANES, LANES)
        copy = pltpu.make_async_copy(
            ref, down_ref.at[:, pl.ds(row, TILE), pl.ds(col, LANES)], sems.at[k]
        )
        copy.start()
        copies.append(copy)
    low = lax.broadcasted_iota(jnp.int32, (TILE, LANES), 1) < LANES // 2
    for k, ref in enumerate(more_refs):
        row = pl.multiple_of(lax.rem(me + k, blocks) * (2 * TILE), 2 * TILE)
        for t in range(ref.shape[0] // 2):
            a = ref[2 * t].astype(F32)
            b = ref[2 * t + 1].astype(F32)
            first = jnp.where(low, a, pltpu.roll(b, LANES // 2, 1))
            second = jnp.where(low, pltpu.roll(a, LANES // 2, 1), b)
            both = jnp.concatenate([first, second], axis=0).astype(BF16)
            up_ref[pl.ds(row, 2 * TILE), t * LANES : (t + 1) * LANES] = both
    for copy in copies:
        copy.wait()


def place(held, more, rows, width):
    peers = held[0].shape[0]
    blocks = len(held)
    return pl.pallas_call(
        functools.partial(place_kernel, blocks),
        out_shape=(
            jax.ShapeDtypeStruct((peers, rows, width), BF16),
            jax.ShapeDtypeStruct((blocks * 2 * TILE, peers * rows), BF16),
        ),
        in_specs=[VM] * (2 * blocks),
        out_specs=(VM, VM),
        scratch_shapes=[pltpu.SemaphoreType.DMA((blocks,))],
        compiler_params=params(16),
        name="place",
    )(*held, *more)


def shrink_kernel(group, rank, x_ref, w_ref, r_ref, *refs):
    *base_refs, out_ref = refs
    peers, wrows, width = w_ref.shape
    toks = x_ref.shape[1]
    chunk = max(1, 256 // wrows)
    per = chunk * wrows // rank
    x = x_ref[...].reshape(group * toks, width)
    names = [r_ref[b].astype(F32) for b in range(group)]
    acc = [[jnp.zeros((rank, toks), F32) for _ in range(2)] for _ in range(group)]
    for c in range(peers // chunk):
        w = w_ref[c * chunk : (c + 1) * chunk].reshape(chunk * wrows, width)
        p = lax.dot_general(w, x, NT, preferred_element_type=F32)
        for j in range(per):
            e = c * per + j
            for b in range(group):
                piece = p[j * rank : (j + 1) * rank, b * toks : (b + 1) * toks]
                for k in range(2):
                    acc[b][k] = jnp.where(names[b][k : k + 1] == e, piece, acc[b][k])
    for b in range(group):
        for k in range(2):
            part = acc[b][k]
            for base in base_refs:
                part = part + base[b, pl.ds(k * rank, rank), :]
            out_ref[b, pl.ds(k * rank, rank), :] = part.astype(out_ref.dtype)


def shrink(tokens, weight, names, half, base, rank, group, dtype):
    chips, toks, width2 = tokens.shape
    width = width2 // 2
    sums = pl.BlockSpec((group, 2 * rank, toks), lambda i: (i, 0, 0))
    return pl.pallas_call(
        functools.partial(shrink_kernel, group, rank),
        grid=(chips // group,),
        out_shape=jax.ShapeDtypeStruct((chips, 2 * rank, toks), dtype),
        in_specs=[
            pl.BlockSpec((group, toks, width), lambda i: (i, 0, half)),
            pl.BlockSpec(weight.shape, lambda i: (0, 0, 0)),
            pl.BlockSpec((group, TILE, LANES), lambda i: (i, 0, 0)),
        ]
        + [sums] * len(base),
        out_specs=sums,
        compiler_params=params(14),
        cost_estimate=pl.CostEstimate(
            flops=2 * chips * toks * width * weight.shape[0] * weight.shape[1],
            bytes_accessed=2 * (chips * toks * width + weight.size),
            transcendentals=0,
        ),
        name="shrink",
    )(tokens, weight, names, *base)


def combine_kernel(peers, rank, part_ref, gate_ref, out_ref):
    gated = []
    for k in range(2):
        total = part_ref[0, pl.ds(k * rank, rank), :].astype(F32)
        for p in range(1, peers):
            total = total + part_ref[p, pl.ds(k * rank, rank), :].astype(F32)
        gated.append((total.astype(BF16).astype(F32) * gate_ref[pl.ds(k, 1), :]).astype(BF16))
    both = jnp.concatenate(gated, axis=1)
    for p in range(peers):
        out_ref[p] = both


def combine(part, gates):
    peers, rank2, toks = part.shape
    rank = rank2 // 2
    return pl.pallas_call(
        functools.partial(combine_kernel, peers, rank),
        out_shape=jax.ShapeDtypeStruct((peers, rank, 2 * toks), BF16),
        in_specs=[VM, VM],
        out_specs=VM,
        compiler_params=params(16),
        name="combine",
    )(part, gates)


def expand_kernel(group, experts, s_ref, r_ref, own_ref, other_ref, out_ref):
    rank = s_ref.shape[1]
    toks = s_ref.shape[2] // 2
    feats = own_ref.shape[0]
    spread = []
    for b in range(group):
        s = s_ref[b]
        names = r_ref[b]
        s0, s1 = s[:, :toks], s[:, toks:]
        r0, r1 = (jnp.broadcast_to(names[k : k + 1], (rank, toks)) for k in range(2))
        zero = jnp.zeros((rank, toks), BF16)
        rows = []
        for e in range(experts):
            name = jnp.asarray(e, BF16)
            rows.append(jnp.where(r0 == name, s0, jnp.where(r1 == name, s1, zero)))
        spread.append(jnp.concatenate(rows, axis=0))
    spread = jnp.concatenate(spread, axis=1)
    for h, w_ref in enumerate((own_ref, other_ref)):
        out = jnp.dot(w_ref[...], spread, preferred_element_type=F32)
        for b in range(group):
            out_ref[b, pl.ds(h * feats, feats), :] = out[:, b * toks : (b + 1) * toks].astype(BF16)


def expand(vectors, names, own, other, rank, group):
    chips, _, toks2 = vectors.shape
    toks = toks2 // 2
    feats, cols = own.shape
    return pl.pallas_call(
        functools.partial(expand_kernel, group, cols // rank),
        grid=(chips // group,),
        out_shape=jax.ShapeDtypeStruct((chips, 2 * feats, toks), BF16),
        in_specs=[
            pl.BlockSpec((group, rank, toks2), lambda i: (i, 0, 0)),
            pl.BlockSpec((group, TILE, LANES), lambda i: (i, 0, 0)),
            pl.BlockSpec(own.shape, lambda i: (0, 0)),
            pl.BlockSpec(other.shape, lambda i: (0, 0)),
        ],
        out_specs=pl.BlockSpec((group, 2 * feats, toks), lambda i: (i, 0, 0)),
        compiler_params=params(24),
        name="expand",
    )(vectors, names, own, other)


def unpack_kernel(blocks, in_ref, out_ref, buf, sems):
    chips, feats2, toks = in_ref.shape
    feats = feats2 // 2
    piece = feats // blocks
    per = LANES // piece // 2
    cols = 2 * chips * piece
    core = lax.rem(lax.axis_index("expert"), 2)
    copies = []
    for z in range(blocks):
        for q in range(chips // per):
            parts = []
            for k in range(per):
                for side in range(2):
                    half = core if side == 0 else 1 - core
                    row = pl.multiple_of(half * feats + z * piece, piece)
                    parts.append(in_ref[per * q + k, pl.ds(row, piece), :])
            buf[z, q] = jnp.concatenate(parts, axis=0).T
            copy = pltpu.make_async_copy(
                buf.at[z, q], out_ref.at[:, pl.ds(z * cols + q * LANES, LANES)], sems.at[z, q]
            )
            copy.start()
            copies.append(copy)
    for copy in copies:
        copy.wait()


def unpack(buf, blocks):
    chips, feats2, toks = buf.shape
    quads = chips * (feats2 // blocks) // LANES
    return pl.pallas_call(
        functools.partial(unpack_kernel, blocks),
        out_shape=jax.ShapeDtypeStruct((toks, chips * feats2), buf.dtype),
        in_specs=[VM],
        out_specs=ANY,
        scratch_shapes=[
            pltpu.VMEM((blocks, quads, toks, LANES), buf.dtype),
            pltpu.SemaphoreType.DMA((blocks, quads)),
        ],
        compiler_params=params(16),
        name="unpack",
    )(buf)


def swap(x):
    return lax.all_to_all(x, "expert", split_axis=0, concat_axis=0, tiled=True)


def swap_chips(x):
    chips = x.shape[0]
    groups = [[2 * q + core for q in range(chips)] for core in range(2)]
    return lax.all_to_all(x, "expert", split_axis=0, concat_axis=0, axis_index_groups=groups, tiled=True)


def sibling(x, peers):
    return lax.ppermute(x, "expert", [(i, i ^ 1) for i in range(peers)])


def ring(x, blocks, turn):
    held = {0: x}
    for step in range(1, blocks // 2 + 1):
        for way in (turn, -turn) if 2 * step < blocks else (turn,):
            pairs = [(i, (i - way) % blocks) for i in range(blocks)]
            held[way * step % blocks] = lax.ppermute(held[way * (step - 1) % blocks], "tensor", pairs)
    return [held[k] for k in range(blocks)]


def per_device(tokens, routes, route_weight, shrink_weight, expand_weight):
    local, rank, features = shrink_weight.shape
    peers = lax.axis_size("expert")
    blocks = lax.axis_size("tensor")
    rows = local * rank
    chips = peers // 2
    group = min(8, chips)
    core = lax.rem(lax.axis_index("expert"), 2)
    first = swap(
        pack_first(shrink_weight.reshape(rows, -1), expand_weight.reshape(rows, -1), routes.T, peers, blocks)
    )
    arrived = swap_chips(pack(tokens, chips))
    names = first.reshape(chips, 2, 3 * TILE, LANES)[:, :, 2 * TILE :]
    names = lax.dynamic_index_in_dim(names, core, 1, keepdims=False)
    downs, ups = ring(first[:, :TILE], blocks, 1), ring(first[:, TILE : 2 * TILE], blocks, -1)
    down, up = place(downs, ups, rows, features // peers)
    other_down, other_up = sibling(down, peers), sibling(up, peers)
    own = shrink(arrived, down, names, 0, [], rank, group, F32)
    partial = shrink(arrived, other_down, names, 1, [own], rank, group, BF16)
    vectors = swap_chips(combine(swap_chips(partial), route_weight.T))
    return unpack(swap_chips(expand(vectors, names, up, other_up, rank, group)), blocks)


def solution(mesh):
    return jax.shard_map(
        per_device,
        mesh=mesh,
        in_specs=(
            P(("expert", "tensor"), None),
            P(("expert", "tensor"), None),
            P(("expert", "tensor"), None),
            P("expert", None, None),
            P("expert", None, "tensor"),
        ),
        out_specs=P(("expert", "tensor"), None),
        check_vma=False,
    )
```
